128 devices in a mesh: dp: 8 (over x, core), list: 16 (over y, z).
Axes of the slice: x: 4, y: 4, z: 4, core: 2. Of those that a mesh axis runs over, the one named last changes fastest.
Arguments:
- vectors: bfloat16 [262144, 768], P(('dp', 'list')), may hold values from -6 to 6
- list_ids: int32 [262144], P(('dp', 'list')), may hold values from 0 to 4095
- codes: int32 [262144, 96], P(('dp', 'list')), may hold values from 0 to 255
- fill_counts: int32 [128, 16], P(('dp', 'list')), may hold values from 1 to 128, as said below
- centroids: bfloat16 [65536, 768], P('list'), may hold values from -6 to 6
- codebooks: float32 [96, 8, 256], replicated, may hold values from -4 to 4
Outputs:
- quant_error: bfloat16 [262144, 768], P(('dp', 'list'))
- new_codebooks: float32 [96, 8, 256], replicated
- gram: float32 [768, 768], replicated
The draws below stay inside these ranges and needn't reach their ends.
Inputs may be any that keep to these rules, and one draw needn't show every extreme that they name: `fill_counts`: every entry is at least 1 and at most 128; in every draw some owner has 128 used slots in the block of every device.
All inputs are finite; a program needn't handle non-finite values.
Results may differ from the reference program's by a relative error of at most 0.0051.
Values may be sent and summed in bfloat16 or wider, within the bound.
A program may use at most 128 MiB of HBM per device.

```python
import math
import jax
import jax.numpy as jnp
import numpy as np
from jax import lax

D = 768
M = 96
SUB = 8
K = 256
LIST_DEV = 4096
SLOTS_DEV = 2048
LISTS = 65536
ROWS = 262144
N_DP = 8
N_LIST = 16


def draw_fill_counts(key, part):
    key = jax.random.fold_in(key, 7)
    first_key, second_key = jax.random.split(key)
    cap = SLOTS_DEV // N_LIST
    counts = jax.random.randint(first_key, (N_DP * N_LIST, N_LIST), 1, cap + 1, dtype=jnp.int32)
    hottest = jax.random.randint(second_key, (), 0, N_LIST, dtype=jnp.int32)
    column = jnp.arange(N_LIST, dtype=jnp.int32)[None, :]
    return jnp.where(column == hottest, cap, counts).astype(jnp.int32)


def set_ends(result, own_key, smallest, largest):
    spot = [jax.random.randint(jax.random.fold_in(own_key, axis), (), 0, length) for axis, length in enumerate(result.shape)]
    longest = result.shape.index(max(result.shape))
    neighbour = spot[:longest] + [(spot[longest] + 1) % result.shape[longest]] + spot[longest + 1:]
    return result.at[tuple(spot)].set(smallest).at[tuple(neighbour)].set(largest)


def block_levels(stream_key, extent, shards, smallest, largest):
    factor_of = 1.0
    for axis_at, blocks in shards:
        draws = jax.random.uniform(jax.random.fold_in(jax.random.fold_in(stream_key, 6), axis_at), (blocks,), jnp.float32, smallest / len(shards), largest / len(shards))
        factor_of = factor_of * jnp.repeat(jnp.exp(draws), extent[axis_at] // blocks).reshape((-1,) + (1,) * (len(extent) - 1 - axis_at))
    return factor_of


def cumulative_ranks(amount, slope):
    portions = [(1 << 20) // math.isqrt(rank ** slope) + 1 for rank in range(1, amount + 1)]
    scale = 1 + sum(portions) // (1 << 30)
    return np.cumsum(np.array([max(1, weight // scale) for weight in portions]))


def ranked(key, dims, number_of, slope):
    listing = cumulative_ranks(number_of, slope)
    ticket = jax.random.randint(jax.random.fold_in(key, 1), dims, 0, int(listing[number_of - 1]))
    standing = jnp.searchsorted(jnp.asarray(listing, jnp.int32), ticket, side="right")
    return jax.random.permutation(jax.random.fold_in(key, 2), number_of)[standing].astype(jnp.int32)


def noise(rng, extent, spread, bound, shards=(), held_as=jnp.bfloat16):
    factor_of = block_levels(rng, extent, shards, -0.22, 0.18) if shards else 1.0
    entries = jax.random.normal(rng, extent, jnp.float32) * spread * factor_of
    return jnp.minimum(jnp.maximum(entries, -bound), bound).astype(held_as)


def setup_inputs(seed: int = 0) -> dict:
    streams_of = jax.random.split(jax.random.key(seed), 7)
    vectors = noise(streams_of[0], (ROWS, D), 1.0, 6.0, ((0, 128),))
    list_ids = set_ends(ranked(streams_of[1], (ROWS,), LIST_DEV, 2), jax.random.fold_in(streams_of[1], 3), 0, LIST_DEV - 1).astype(jnp.int32)
    codes = set_ends(jax.random.randint(streams_of[2], (ROWS, M), 0, K), jax.random.fold_in(streams_of[2], 1), 0, K - 1).astype(jnp.int32)
    fill_counts = draw_fill_counts(jax.random.fold_in(streams_of[6], 71), 0)
    centroids = noise(streams_of[4], (LISTS, D), 1.0, 6.0, ((0, 16),))
    codebooks = noise(streams_of[5], (M, SUB, K), 0.5, 4.0, (), jnp.float32)
    return {"vectors": vectors, "list_ids": list_ids, "codes": codes, "fill_counts": fill_counts, "centroids": centroids, "codebooks": codebooks}


def reference(vectors, list_ids, codes, fill_counts, centroids, codebooks):
    cap = SLOTS_DEV // N_LIST
    devices_all = N_DP * N_LIST
    owner = (jnp.arange(SLOTS_DEV, dtype=jnp.int32) // cap).astype(jnp.int32)
    place = (jnp.arange(SLOTS_DEV, dtype=jnp.int32) % cap).astype(jnp.int32)
    kinds = jnp.arange(K, dtype=jnp.int32)

    def residual_of(index):
        start = (index * SLOTS_DEV).astype(jnp.int32)
        block = lax.dynamic_slice_in_dim(vectors, start, SLOTS_DEV, 0)
        wanted = lax.dynamic_slice_in_dim(list_ids, start, SLOTS_DEV, 0)
        code_rows = lax.dynamic_slice_in_dim(codes, start, SLOTS_DEV, 0)
        rows = jnp.take(centroids, owner * LIST_DEV + wanted, axis=0)
        diff = (block.astype(jnp.float32) - rows.astype(jnp.float32)).astype(jnp.bfloat16)
        live = (place < fill_counts[index][owner]).astype(jnp.bfloat16)
        return diff * live[:, None], live, code_rows

    def first(carry, index):
        gram_acc, sums, counts = carry
        diff, live, code_rows = residual_of(index)
        gram_acc = gram_acc + jnp.dot(diff.T, diff, preferred_element_type=jnp.float32)
        onehot = (code_rows[:, :, None] == kinds).astype(jnp.float32) * live.astype(jnp.float32)[:, None, None]
        sums = sums + jnp.einsum("rmd,rmk->mdk", diff.astype(jnp.float32).reshape(SLOTS_DEV, M, SUB), onehot, precision=lax.Precision.HIGHEST)
        counts = counts + jnp.sum(onehot, axis=0)
        return (gram_acc, sums, counts), None

    start_carry = (jnp.zeros((D, D), jnp.float32), jnp.zeros((M, SUB, K), jnp.float32), jnp.zeros((M, K), jnp.float32))
    (gram_acc, sums, counts), unused = lax.scan(first, start_carry, jnp.arange(devices_all, dtype=jnp.int32))
    new_books = (sums + codebooks) / (counts[:, None, :] + 1.0)
    books_turned = jnp.transpose(new_books, (0, 2, 1))
    subspace_ids = jnp.arange(M, dtype=jnp.int32)[None, :]

    def second(carry, index):
        diff, live, code_rows = residual_of(index)
        recon = books_turned[subspace_ids, code_rows].reshape(SLOTS_DEV, D)
        error = (diff.astype(jnp.float32) - recon) * live.astype(jnp.float32)[:, None]
        return carry, error.astype(jnp.bfloat16)

    unused, errors = lax.scan(second, 0, jnp.arange(devices_all, dtype=jnp.int32))
    total = float(SLOTS_DEV * devices_all)
    return errors.reshape(SLOTS_DEV * devices_all, D), new_books, gram_acc / total
```

```python
import functools

import jax
import jax.numpy as jnp
from jax import lax
from jax.experimental import pallas as pl
from jax.experimental.pallas import tpu as pltpu
from jax.sharding import PartitionSpec as P

MESH = pl.DeviceIdType.MESH
F32 = jnp.float32
BF = jnp.bfloat16
NL, ND = 16, 8
CAP = 128
SLOTS = NL * CAP
NC = 6
CW = 128
MC = 16
GROUPS = ((0, 1, 2), (3, 4), (5,))
GSTEP = 512


def sum_rows(g):
    return len(GROUPS[g]) * 24


def block_of(j, i):
    return j * (j + 1) // 2 + i


def drain(ref, sem):
    pltpu.make_async_copy(ref, ref, sem).wait()


def refine_kernel(
    ids_ref, fill_ref, vec_hbm, codes_hbm, cent_hbm, books_hbm,
    rest_hbm, nb0_hbm, nb1_hbm, nb2_hbm, ga_hbm, gb_hbm,
    ids_in, ids_s, table, cbuf, gbuf, sbuf, rbuf, vec, codes, books, res, rest, live, acc,
    ds0, ds1, ds2, dr0, dr1, dr2, ls0, ls1, ls2, lr0, lr1, lr2,
    as0, as1, as2, ad0, ad1, ad2,
    gsa, gsb, gra, grb, gla, glb, gma, gmb, gta, gtb, gda, gdb,
    load_sem, cent_sem, out_sem, ids_ssem, ids_rsem, self_sem, x_ssem, x_rsem,
    ar_ssem, ar_rsem,
):
    dp = lax.axis_index("dp")
    me = lax.axis_index("list")
    my_y, my_z = me // 4, me % 4

    def list_peer(s):
        return lax.rem(my_y + s // 4, 4) * 4 + lax.rem(my_z + s % 4, 4)

    def dp_peer(s):
        return lax.rem(dp + s, ND)

    cent_rows = cbuf.shape[1]
    n_cent = cent_hbm.shape[0] // cent_rows

    def cent_copy(b):
        slot = lax.rem(b, 2)
        return pltpu.make_async_copy(
            cent_hbm.at[pl.ds(b * cent_rows, cent_rows)], cbuf.at[slot], cent_sem.at[slot])

    codes_load = pltpu.make_async_copy(codes_hbm, codes, load_sem.at[0])
    books_load = pltpu.make_async_copy(books_hbm, books, load_sem.at[1])
    vec_load = pltpu.make_async_copy(vec_hbm, vec, load_sem.at[2])
    cent_copy(0).start()
    cent_copy(1).start()

    barrier = pltpu.get_barrier_semaphore()

    def greet_list(s, c):
        pl.semaphore_signal(barrier, inc=1, device_id={"list": list_peer(s)}, device_id_type=MESH)
        return c

    def greet_dp(s, c):
        pl.semaphore_signal(barrier, inc=1, device_id={"dp": dp_peer(s)}, device_id_type=MESH)
        return c

    lax.fori_loop(1, NL, greet_list, 0)
    lax.fori_loop(1, ND, greet_dp, 0)
    pl.semaphore_wait(barrier, NL + ND - 2)

    def send_ids(s, c):
        p = list_peer(s)
        pltpu.make_async_remote_copy(
            src_ref=ids_ref.at[p], dst_ref=ids_in.at[me], send_sem=ids_ssem, recv_sem=ids_rsem,
            device_id={"list": p}, device_id_type=MESH).start()
        return c

    lax.fori_loop(1, NL, send_ids, 0)
    vec_load.start()
    codes_load.start()
    books_load.start()
    ids_in[me] = ids_ref[me]

    table_rows = table.reshape(4096 * 8, 128)
    gathered_rows = gbuf.reshape(CAP * 8, 128)

    def build(b, c):
        cent_copy(b).wait()
        slot = lax.rem(b, 2)

        def rows16(r, c):
            for j in range(NC):
                v = cbuf[slot, pl.ds(pl.multiple_of(r * 16, 16), 16), j * CW:(j + 1) * CW].astype(F32)
                base = (b * cent_rows + r * 16) * 8
                table_rows[pl.ds(base + j, 8, stride=8), :] = v[:8]
                table_rows[pl.ds(base + 64 + j, 8, stride=8), :] = v[8:]
            return c

        lax.fori_loop(0, cent_rows // 16, rows16, 0)

        @pl.when(b + 2 < n_cent)
        def _():
            cent_copy(b + 2).start()

        return c

    lax.fori_loop(0, n_cent, build, 0)

    drain(ids_in.at[pl.ds(0, NL - 1)], ids_rsem)
    drain(ids_in.at[pl.ds(0, NL - 1)], ids_ssem)
    to_smem = pltpu.make_async_copy(ids_in, ids_s, self_sem)
    to_smem.start()
    to_smem.wait()

    def x_copy(j, p):
        return pltpu.make_async_remote_copy(
            src_ref=sbuf.at[j, p], dst_ref=rbuf.at[j, me], send_sem=x_ssem, recv_sem=x_rsem.at[j],
            device_id={"list": p}, device_id_type=MESH)

    def gather(p):
        def rows(r, c):
            for k in range(16):
                at = r * 16 + k
                row = ids_s[p, 0, at]
                gbuf[at] = table[row]
            return c

        lax.fori_loop(0, CAP // 16, rows, 0)

        def pack(r, c):
            for j in range(NC):
                lo = gathered_rows[pl.ds(r * 128 + j, 8, stride=8), :]
                hi = gathered_rows[pl.ds(r * 128 + 64 + j, 8, stride=8), :]
                sbuf[j, p, pl.ds(pl.multiple_of(r * 16, 16), 16), :] = jnp.concatenate([lo, hi], 0).astype(BF)
            return c

        lax.fori_loop(0, CAP // 16, pack, 0)

    def gather_send(s, c):
        p = list_peer(s)
        gather(p)
        x_copy(0, p).start()
        return c

    lax.fori_loop(1, NL, gather_send, 0)

    def send_chunk(j, c):
        def one(s, c):
            x_copy(j, list_peer(s)).start()
            return c

        return lax.fori_loop(1, NL, one, c)

    lax.fori_loop(1, NC, send_chunk, 0)
    gather(me)

    def own(j, c):
        def rows(r, c):
            at = pl.ds(pl.multiple_of(r * 16, 16), 16)
            rbuf[j, me, at, :] = sbuf[j, me, at, :]
            return c

        return lax.fori_loop(0, CAP // 16, rows, c)

    lax.fori_loop(0, NC, own, 0)

    lane = lax.broadcasted_iota(jnp.int32, (16, CAP), 1)
    for p in range(NL):
        live[:, p * CAP:(p + 1) * CAP] = (lane < fill_ref[0, p]).astype(F32).astype(BF)

    vec_load.wait()
    codes_load.wait()
    books_load.wait()

    send_sums = (ds0, ds1, ds2)
    lane128 = lax.broadcasted_iota(jnp.int32, (8, 128), 1)
    row8 = lax.broadcasted_iota(jnp.int32, (8, 128), 0)
    sub16 = lax.broadcasted_iota(jnp.int32, (16, GSTEP), 0)
    sub16_f = sub16.astype(F32).astype(BF)
    sub16_h = (sub16 // 4).astype(F32).astype(BF)

    def residual_chunk(j):
        def one(p, c):
            rows = pl.ds(pl.multiple_of(p * CAP, CAP), CAP)
            v = vec[rows, pl.ds(pl.multiple_of(j * CW, CW), CW)].astype(F32)
            d = v - rbuf[j, p].astype(F32)
            keep = lax.broadcasted_iota(jnp.int32, (CAP, CW), 0) < fill_ref[0, p]
            d = jnp.where(keep, d, 0.0).astype(BF)
            res[j, rows, :] = d
            rest[j, :, pl.ds(pl.multiple_of(p * CAP, CAP), CAP)] = d.T
            return c

        lax.fori_loop(0, NL, one, 0)

    def hist_chunk(g, u, j):
        acc[...] = jnp.zeros_like(acc)

        def step(t, c):
            gs = pl.ds(pl.multiple_of(t * GSTEP, GSTEP), GSTEP)
            code = codes[j, :, gs]
            hi_all = (code >> 6).astype(F32)
            lo_all = (code & 63).astype(F32)
            alive = live[:, gs]
            zero = jnp.zeros((16, GSTEP), BF)
            one = jnp.ones((16, GSTEP), BF)
            for grp in range(4):
                left = []
                for pair in range(2):
                    m = grp * 4 + pair * 2
                    hi2 = jnp.concatenate([
                        jnp.broadcast_to(hi_all[m:m + 1], (8, GSTEP)),
                        jnp.broadcast_to(hi_all[m + 1:m + 2], (8, GSTEP))], 0).astype(BF)
                    r16 = rest[j, m * 8:m * 8 + 16, gs]
                    for h in range(4):
                        left.append(jnp.where(hi2 == jnp.array(h, BF), r16, zero))
                hi4 = hi_all[grp * 4:grp * 4 + 4]
                hi4 = jnp.concatenate([hi4, hi4, hi4, hi4], 0).astype(BF)
                left.append(jnp.where(hi4 == sub16_h, alive, zero))
                right = []
                for ml in range(4):
                    m = grp * 4 + ml
                    lo = jnp.broadcast_to(lo_all[m:m + 1], (16, GSTEP)).astype(BF)
                    for t16 in range(4):
                        right.append(jnp.where(lo == sub16_f + jnp.array(16 * t16, BF), one, zero))
                acc[grp] += lax.dot_general(
                    jnp.concatenate(left, 0), jnp.concatenate(right, 0),
                    (((1,), (1,)), ((), ())), preferred_element_type=F32)
            return c

        lax.fori_loop(0, SLOTS // GSTEP, step, 0)
        buf = send_sums[g]
        base = pl.multiple_of(u * 24, 8)
        for grp in range(4):
            for pair in range(2):
                q = grp * 2 + pair
                tile = slice(pair * 128, pair * 128 + 128)
                for t in range(2):
                    out = slice(t * 128, t * 128 + 128)
                    cnt = []
                    for m2 in range(2):
                        halves = []
                        for h, here in ((2 * t, m2 == 0), (2 * t + 1, m2 == 1)):
                            at = pair * 64 + h * 16 + m2 * 8
                            row = 128 + h * 4 + pair * 2 + m2
                            s = acc[grp, at:at + 8, tile]
                            n = jnp.broadcast_to(acc[grp, row:row + 1, tile], (8, 128))
                            if not here:
                                s = pltpu.roll(s, 64, 1)
                                n = pltpu.roll(n, 64, 1)
                            halves.append((s, n))
                        buf[q, pl.ds(base + m2 * 8, 8), out] = jnp.where(lane128 < 64, halves[0][0], halves[1][0])
                        cnt.append(jnp.where(lane128 < 64, halves[0][1], halves[1][1]))
                    buf[q, pl.ds(base + 16, 8), out] = jnp.where(row8 == 0, cnt[0], cnt[1])

    def gram_chunk(buf, j, first):
        def one(i, c):
            block = lax.dot_general(
                rest[j], res[i], (((1,), (0,)), ((), ())), preferred_element_type=F32) * (1.0 / (SLOTS * NL * ND))
            for q in range(ND):
                buf[q, first + i] = block[q * 16:q * 16 + 16].astype(BF)
            return c

        lax.fori_loop(0, j + 1, one, 0)

    def start_dp(a, src, dst):
        def one(s, c):
            q = dp_peer(s)
            pltpu.make_async_remote_copy(
                src_ref=src.at[q], dst_ref=dst.at[dp], send_sem=ar_ssem.at[a, 0], recv_sem=ar_rsem.at[a, 0],
                device_id={"dp": q}, device_id_type=MESH).start()
            return c

        lax.fori_loop(1, ND, one, 0)

    def start_list(a, src, dst):
        def one(s, c):
            p = list_peer(s)
            pltpu.make_async_remote_copy(
                src_ref=src.at[p], dst_ref=dst.at[me], send_sem=ar_ssem.at[a, 1], recv_sem=ar_rsem.at[a, 1],
                device_id={"list": p}, device_id_type=MESH).start()
            return c

        lax.fori_loop(1, NL, one, 0)

    def share_list(a, buf):
        def one(s, c):
            pltpu.make_async_remote_copy(
                src_ref=buf.at[me], dst_ref=buf.at[me], send_sem=ar_ssem.at[a, 2], recv_sem=ar_rsem.at[a, 2],
                device_id={"list": list_peer(s)}, device_id_type=MESH).start()
            return c

        lax.fori_loop(1, NL, one, 0)

    def share_dp(a, buf):
        def one(s, c):
            pltpu.make_async_remote_copy(
                src_ref=buf.at[dp], dst_ref=buf.at[dp], send_sem=ar_ssem.at[a, 3], recv_sem=ar_rsem.at[a, 3],
                device_id={"dp": dp_peer(s)}, device_id_type=MESH).start()
            return c

        lax.fori_loop(1, ND, one, 0)

    recv_sums, ls, lr, ag, ad = (dr0, dr1, dr2), (ls0, ls1, ls2), (lr0, lr1, lr2), (as0, as1, as2), (ad0, ad1, ad2)

    def sums_1(g):
        start_dp(g, send_sums[g], recv_sums[g])

    def sums_2(g):
        src, dst, width = send_sums[g], recv_sums[g], len(GROUPS[g])
        drain(dst.at[pl.ds(0, ND - 1)], ar_rsem.at[g, 0])
        dst[dp] = src[dp]
        total = dst[0]
        for q in range(1, ND):
            total = total + dst[q]
        for u in range(width):
            for p in range(NL):
                ls[g][p, u:u + 1, :] = total[u * 24 + p:u * 24 + p + 1]
                at = u * 24 + 16 + p // 8
                ls[g][p, width + u:width + u + 1, :] = total[at:at + 1]
        start_list(g, ls[g], lr[g])

    def sums_3(g):
        width = len(GROUPS[g])
        drain(lr[g].at[pl.ds(0, NL - 1)], ar_rsem.at[g, 1])
        lr[g][me] = ls[g][me]
        total = lr[g][0]
        for p in range(1, NL):
            total = total + lr[g][p]
        for u in range(width):
            m = GROUPS[g][u] * MC + dp * 2 + me // 8
            old = books[m, pl.ds(lax.rem(me, 8), 1), :]
            ag[g][me, u:u + 1, :] = (total[u:u + 1] + old) / (total[width + u:width + u + 1] + 1.0)
        share_list(g, ag[g])

    def sums_4(g):
        drain(ag[g].at[pl.ds(0, NL - 1)], ar_rsem.at[g, 2])
        for u in range(len(GROUPS[g])):
            for p in range(NL):
                ad[g][dp, u, p:p + 1, :] = ag[g][p, u:u + 1, :]
        share_dp(g, ad[g])

    def sums_5(g):
        drain(ad[g].at[pl.ds(0, ND - 1)], ar_rsem.at[g, 3])

    gs_, gr_, gl_, gm_, gt_, gd_ = (gsa, gsb), (gra, grb), (gla, glb), (gma, gmb), (gta, gtb), (gda, gdb)

    def gram_1(k):
        start_dp(3 + k, gs_[k], gr_[k])

    def gram_2(k):
        drain(gr_[k].at[pl.ds(0, ND - 1)], ar_rsem.at[3 + k, 0])
        blocks = gs_[k].shape[1]

        def one(b, c):
            total = gs_[k][dp, b].astype(F32)
            for s in range(1, ND):
                total = total + gr_[k][dp_peer(s), b].astype(F32)
            gl_[k][b] = total.astype(BF)
            return c

        lax.fori_loop(0, blocks, one, 0)
        for b in range(blocks, NL):
            gl_[k][b] = jnp.zeros((16, CW), BF)
        start_list(3 + k, gl_[k], gm_[k])

    def gram_3(k):
        drain(gm_[k].at[pl.ds(0, NL - 1)], ar_rsem.at[3 + k, 1])
        total = gl_[k][me].astype(F32)
        for s in range(1, NL):
            total = total + gm_[k][list_peer(s)].astype(F32)
        gt_[k][me] = total.astype(BF)
        share_list(3 + k, gt_[k])

    def gram_4(k):
        drain(gt_[k].at[pl.ds(0, NL - 1)], ar_rsem.at[3 + k, 2])
        gd_[k][dp] = gt_[k][...]
        share_dp(3 + k, gd_[k])

    def gram_5(k):
        drain(gd_[k].at[pl.ds(0, ND - 1)], ar_rsem.at[3 + k, 3])

    def rest_out(j):
        return pltpu.make_async_copy(rest.at[j], rest_hbm.at[j], out_sem.at[0])

    def chunk(g, u, j):
        drain(rbuf.at[j, pl.ds(0, NL - 1)], x_rsem.at[j])
        residual_chunk(j)
        hist_chunk(g, u, j)

    def group(g):
        first = GROUPS[g][0]

        def one(u, c):
            chunk(g, u, first + u)
            gram_chunk(gsa, first + u, block_of(first + u, 0))
            return c

        lax.fori_loop(0, len(GROUPS[g]), one, 0)

    group(0)
    sums_1(0)
    group(1)
    sums_1(1)
    gram_1(0)
    sums_2(0)
    chunk(2, 0, NC - 1)
    sums_1(2)
    sums_2(1)
    gram_2(0)
    sums_3(0)
    gram_chunk(gsb, NC - 1, 0)
    gram_1(1)
    sums_2(2)
    sums_3(1)
    gram_3(0)
    sums_4(0)
    gram_2(1)
    sums_3(2)
    sums_4(1)
    gram_4(0)
    gram_3(1)
    sums_4(2)
    gram_4(1)
    for g in range(3):
        sums_5(g)
    for k in range(2):
        gram_5(k)
    outs = [pltpu.make_async_copy(s, d, out_sem.at[i]) for i, (s, d) in enumerate(
        ((rest, rest_hbm), (ad0, nb0_hbm), (ad1, nb1_hbm), (ad2, nb2_hbm), (gda, ga_hbm), (gdb, gb_hbm)))]
    for o in outs:
        o.start()
    for j in range(NC):
        drain(sbuf.at[j, pl.ds(0, NL - 1)], x_ssem)
    for g in range(3):
        drain(send_sums[g].at[pl.ds(0, ND - 1)], ar_ssem.at[g, 0])
        drain(ls[g].at[pl.ds(0, NL - 1)], ar_ssem.at[g, 1])
        drain(ag[g].at[pl.ds(0, NL - 1)], ar_ssem.at[g, 2])
        drain(ad[g].at[pl.ds(0, ND - 1)], ar_ssem.at[g, 3])
    for k in range(2):
        drain(gs_[k].at[pl.ds(0, ND - 1)], ar_ssem.at[3 + k, 0])
        drain(gl_[k].at[pl.ds(0, NL - 1)], ar_ssem.at[3 + k, 1])
        drain(gt_[k].at[pl.ds(0, NL - 1)], ar_ssem.at[3 + k, 2])
        drain(gd_[k].at[pl.ds(0, ND - 1)], ar_ssem.at[3 + k, 3])
    for o in outs:
        o.wait()


def refine(ids, fill, vectors, codes, centroids, codebooks):
    anyspace = pl.BlockSpec(memory_space=pl.ANY)
    V = pltpu.VMEM
    widths = [len(g) for g in GROUPS]
    blocks = (15, 6)
    dma = pltpu.SemaphoreType.DMA
    out_shape = (
        [jax.ShapeDtypeStruct((NC, CW, SLOTS), BF)]
        + [jax.ShapeDtypeStruct((ND, w, NL, 256), F32) for w in widths]
        + [jax.ShapeDtypeStruct((ND, NL, 16, CW), BF) for _ in blocks]
    )
    scratch = (
        [
            V((NL, 1, CAP), jnp.int32), pltpu.SMEM((NL, 1, CAP), jnp.int32),
            V((4096, 8, 128), F32), V((2, 256, 768), BF), V((CAP, 8, 128), F32),
            V((NC, NL, CAP, CW), BF), V((NC, NL, CAP, CW), BF),
            V((SLOTS, 768), BF), V((NC, MC, SLOTS), jnp.int32), V((96, 8, 256), F32),
            V((NC, SLOTS, CW), BF), V((NC, CW, SLOTS), BF), V((16, SLOTS), BF), V((4, 144, 256), F32),
        ]
        + [V((ND, sum_rows(g), 256), F32) for g in range(3)] * 2
        + [V((NL, 2 * w, 256), F32) for w in widths] * 2
        + [V((NL, w, 256), F32) for w in widths]
        + [V((ND, w, NL, 256), F32) for w in widths]
        + [V((ND, b, 16, CW), BF) for b in blocks] * 2
        + [V((NL, 16, CW), BF) for _ in blocks] * 3
        + [V((ND, NL, 16, CW), BF) for _ in blocks]
        + [dma((3,)), dma((2,)), dma((6,)), dma, dma, dma, dma, dma((NC,)), dma((5, 4)), dma((5, 4))]
    )
    return pl.pallas_call(
        refine_kernel,
        out_shape=out_shape,
        in_specs=[pl.BlockSpec(memory_space=pltpu.VMEM), pl.BlockSpec(memory_space=pltpu.SMEM)] + [anyspace] * 4,
        out_specs=[anyspace] * 6,
        scratch_shapes=scratch,
        compiler_params=pltpu.CompilerParams(
            collective_id=0, has_side_effects=True, vmem_limit_bytes=60 << 20),
    )(ids, fill, vectors, codes, centroids, codebooks)


def error_kernel(fill_ref, rest_ref, codes_ref, nb0, nb1, nb2, ga, gb, err_ref, books_ref, gram_ref):
    step = pl.program_id(0)
    nb = (nb0, nb1, nb2)

    @pl.when(step == 0)
    def _():
        for g in range(3):
            for u, j in enumerate(GROUPS[g]):
                for q in range(ND):
                    for m2 in range(2):
                        books_ref[j * MC + q * 2 + m2] = nb[g][q, u, m2 * 8:m2 * 8 + 8, :]

    @pl.when(step == 1)
    def _():
        for j in range(NC):
            for i in range(j + 1):
                src, b = (ga, block_of(j, i)) if j < NC - 1 else (gb, i)
                block = jnp.concatenate([src[q, b].astype(F32) for q in range(ND)], 0)
                gram_ref[j * CW:(j + 1) * CW, i * CW:(i + 1) * CW] = block
                if i < j:
                    gram_ref[i * CW:(i + 1) * CW, j * CW:(j + 1) * CW] = block.T

    lane = lax.broadcasted_iota(jnp.int32, (8, 128), 1)
    used = lane < fill_ref[0, step]
    for g in range(3):
        for u, j in enumerate(GROUPS[g]):
            parts = []
            for m in range(MC):
                code = jnp.broadcast_to(codes_ref[j, m:m + 1, :], (8, 128))
                at = code & 127
                t = nb[g][m // 2, u, (m % 2) * 8:(m % 2) * 8 + 8, :]
                lo = jnp.take_along_axis(t[:, :128], at, axis=1, mode="promise_in_bounds")
                hi = jnp.take_along_axis(t[:, 128:], at, axis=1, mode="promise_in_bounds")
                parts.append(jnp.where(code < 128, lo, hi))
            r = rest_ref[j].astype(F32)
            e = r - jnp.concatenate(parts, 0)
            e = jnp.where(jnp.concatenate([used] * MC, 0), e, 0.0)
            err_ref[:, j * CW:(j + 1) * CW] = e.astype(BF).T


def local(vectors, list_ids, codes, fill_counts, centroids, codebooks):
    codes_t = codes.T.reshape(NC, MC, SLOTS)
    rest, nb0, nb1, nb2, ga, gb = refine(
        list_ids.reshape(NL, 1, CAP), fill_counts, vectors, codes_t, centroids, codebooks)
    whole = pl.BlockSpec(memory_space=pltpu.VMEM)
    err, books, gram = pl.pallas_call(
        error_kernel,
        grid=(NL,),
        out_shape=[
            jax.ShapeDtypeStruct((SLOTS, 768), BF),
            jax.ShapeDtypeStruct((96, 8, 256), F32),
            jax.ShapeDtypeStruct((768, 768), F32),
        ],
        in_specs=[
            pl.BlockSpec(memory_space=pltpu.SMEM),
            pl.BlockSpec((NC, CW, CAP), lambda i: (0, 0, i)),
            pl.BlockSpec((NC, MC, CAP), lambda i: (0, 0, i)),
        ] + [whole] * 5,
        out_specs=[
            pl.BlockSpec((CAP, 768), lambda i: (i, 0)),
            whole,
            whole,
        ],
        compiler_params=pltpu.CompilerParams(vmem_limit_bytes=40 << 20),
    )(fill_counts, rest, codes_t, nb0, nb1, nb2, ga, gb)
    return err, books, gram


def solution(mesh):
    in_specs = (
        P(("dp", "list"), None),
        P(("dp", "list")),
        P(("dp", "list"), None),
        P(("dp", "list"), None),
        P("list", None),
        P(),
    )
    out_specs = (P(("dp", "list"), None), P(), P())
    return jax.shard_map(local, mesh=mesh, in_specs=in_specs, out_specs=out_specs, check_vma=False)
```

```python
import functools

import jax
import jax.numpy as jnp
from jax import lax
from jax.experimental import pallas as pl
from jax.experimental.pallas import tpu as pltpu
from jax.sharding import PartitionSpec as P

MESH = pl.DeviceIdType.MESH
F32 = jnp.float32
BF = jnp.bfloat16
NL, ND = 16, 8
CAP = 128
SLOTS = NL * CAP
NC = 6
CW = 128
MC = 16
GROUPS = ((0, 1), (2, 3, 4), (5,))
GSTEP = 1024
AHEAD = 2


def sum_rows(g):
    return len(GROUPS[g]) * 24


def block_of(j, i):
    return j * (j + 1) // 2 + i


def drain(ref, sem):
    pltpu.make_async_copy(ref, ref, sem).wait()


def refine_kernel(
    ids_ref, fill_ref, vec_hbm, codes_hbm, cent_hbm, books_hbm,
    err_hbm, nb_hbm, gram_hbm,
    ids_in, ids_s, table, cbuf, gbuf, sbuf, rbuf, vec, codes, books, res, rest, live, acc, err, gram,
    ds0, ds1, ds2, dr0, dr1, dr2, ls0, ls1, ls2, lr0, lr1, lr2,
    as0, as1, as2, ad0, ad1, ad2,
    gsa, gsb, gra, grb, gla, glb, gma, gmb, gta, gtb, gda, gdb,
    load_sem, cent_sem, out_sem, ids_ssem, ids_rsem, self_sem, x_ssem, x_rsem,
    ar_ssem, ar_rsem,
):
    dp = lax.axis_index("dp")
    me = lax.axis_index("list")
    my_y, my_z = me // 4, me % 4

    def list_peer(s):
        return lax.rem(my_y + s // 4, 4) * 4 + lax.rem(my_z + s % 4, 4)

    def dp_peer(s):
        return lax.rem(dp + s, ND)

    n_cent = cent_sem.shape[0]
    cent_rows = cbuf.shape[0] // n_cent

    def cent_copy(b):
        rows = pl.ds(pl.multiple_of(b * cent_rows, cent_rows), cent_rows)
        return pltpu.make_async_copy(cent_hbm.at[rows], cbuf.at[rows], cent_sem.at[b])

    codes_load = pltpu.make_async_copy(codes_hbm, codes, load_sem.at[0])
    books_load = pltpu.make_async_copy(books_hbm, books, load_sem.at[1])
    vec_load = pltpu.make_async_copy(vec_hbm, vec, load_sem.at[2])
    for b in range(n_cent):
        cent_copy(b).start()
    vec_load.start()
    codes_load.start()
    books_load.start()

    barrier = pltpu.get_barrier_semaphore()

    def greet_list(s, c):
        pl.semaphore_signal(barrier, inc=1, device_id={"list": list_peer(s)}, device_id_type=MESH)
        return c

    def greet_dp(s, c):
        pl.semaphore_signal(barrier, inc=1, device_id={"dp": dp_peer(s)}, device_id_type=MESH)
        return c

    lax.fori_loop(1, NL, greet_list, 0)
    lax.fori_loop(1, ND, greet_dp, 0)

    def send_ids(s, c):
        p = list_peer(s)
        pltpu.make_async_remote_copy(
            src_ref=ids_ref.at[p], dst_ref=ids_in.at[me], send_sem=ids_ssem, recv_sem=ids_rsem,
            device_id={"list": p}, device_id_type=MESH).start()
        return c


    table_rows = table.reshape(4096 * 8, 128)
    gathered_rows = gbuf.reshape(32 * 8, 128)

    def build(b, c):
        cent_copy(b).wait()

        def rows16(r, c):
            row = pl.multiple_of(b * cent_rows + r * 16, 16)
            for j in range(NC):
                v = cbuf[pl.ds(row, 16), j * CW:(j + 1) * CW].astype(F32)
                table_rows[pl.ds(row * 8 + j, 8, stride=8), :] = v[:8]
                table_rows[pl.ds(row * 8 + 64 + j, 8, stride=8), :] = v[8:]
            return c

        return lax.fori_loop(0, cent_rows // 16, rows16, c, unroll=4)

    lax.fori_loop(0, n_cent, build, 0)
    pl.semaphore_wait(barrier, NL + ND - 2)
    lax.fori_loop(1, NL, send_ids, 0)
    ids_in[me] = ids_ref[me]

    lane = lax.broadcasted_iota(jnp.int32, (16, CAP), 1)
    for p in range(NL):
        live[:, p * CAP:(p + 1) * CAP] = (lane < fill_ref[0, p]).astype(F32).astype(BF)

    drain(ids_in.at[pl.ds(0, NL - 1)], ids_rsem)
    drain(ids_in.at[pl.ds(0, NL - 1)], ids_ssem)
    to_smem = pltpu.make_async_copy(ids_in, ids_s, self_sem)
    to_smem.start()
    to_smem.wait()

    def x_copy(j, p):
        return pltpu.make_async_remote_copy(
            src_ref=sbuf.at[j, p], dst_ref=rbuf.at[j, me], send_sem=x_ssem, recv_sem=x_rsem.at[j],
            device_id={"list": p}, device_id_type=MESH)

    def gather(p, dst):
        def rows(r, c):
            for half in range(2):
                for k in range(16):
                    row = ids_s[p, 0, r * 32 + half * 16 + k]
                    gbuf[half * 16 + k] = table[row]
            for half in range(2):
                at = pl.ds(pl.multiple_of(r * 32 + half * 16, 16), 16)
                for j in range(NC):
                    lo = gathered_rows[pl.ds(half * 128 + j, 8, stride=8), :]
                    hi = gathered_rows[pl.ds(half * 128 + 64 + j, 8, stride=8), :]
                    dst[j, p, at, :] = jnp.concatenate([lo, hi], 0).astype(BF)
            return c

        lax.fori_loop(0, CAP // 32, rows, 0)

    def gather_send(s, c):
        p = list_peer(s)
        gather(p, sbuf)
        for j in range(AHEAD):
            x_copy(j, p).start()
        return c

    lax.fori_loop(1, NL, gather_send, 0)

    def send_chunk(j):
        def one(s, c):
            x_copy(j, list_peer(s)).start()
            return c

        lax.fori_loop(1, NL, one, 0)

    gather(me, rbuf)

    vec_load.wait()
    codes_load.wait()
    books_load.wait()

    send_sums = (ds0, ds1, ds2)
    lane128 = lax.broadcasted_iota(jnp.int32, (8, 128), 1)
    row8 = lax.broadcasted_iota(jnp.int32, (8, 128), 0)
    sub16 = lax.broadcasted_iota(jnp.int32, (16, GSTEP), 0)
    sub16_f = sub16.astype(F32).astype(BF)
    sub16_h = (sub16 // 4).astype(F32).astype(BF)

    def residual_chunk(j):
        def one(p, c):
            rows = pl.ds(pl.multiple_of(p * CAP, CAP), CAP)
            v = vec[rows, pl.ds(pl.multiple_of(j * CW, CW), CW)].astype(F32)
            d = v - rbuf[j, p].astype(F32)
            keep = lax.broadcasted_iota(jnp.int32, (CAP, CW), 0) < fill_ref[0, p]
            d = jnp.where(keep, d, 0.0).astype(BF)
            res[j, rows, :] = d
            rest[j, :, pl.ds(pl.multiple_of(p * CAP, CAP), CAP)] = d.T
            return c

        lax.fori_loop(0, NL, one, 0, unroll=4)

    def hist_chunk(g, u, j):
        acc[...] = jnp.zeros_like(acc)

        def step(t, c):
            gs = pl.ds(pl.multiple_of(t * GSTEP, GSTEP), GSTEP)
            code = codes[j, :, gs]
            hi_all = (code >> 6).astype(F32)
            lo_all = (code & 63).astype(F32)
            alive = live[:, gs]
            zero = jnp.zeros((16, GSTEP), BF)
            one = jnp.ones((16, GSTEP), BF)
            for grp in range(4):
                left = []
                for pair in range(2):
                    m = grp * 4 + pair * 2
                    hi2 = jnp.concatenate([
                        jnp.broadcast_to(hi_all[m:m + 1], (8, GSTEP)),
                        jnp.broadcast_to(hi_all[m + 1:m + 2], (8, GSTEP))], 0).astype(BF)
                    r16 = rest[j, m * 8:m * 8 + 16, gs]
                    for h in range(4):
                        left.append(jnp.where(hi2 == jnp.array(h, BF), r16, zero))
                hi4 = hi_all[grp * 4:grp * 4 + 4]
                hi4 = jnp.concatenate([hi4, hi4, hi4, hi4], 0).astype(BF)
                left.append(jnp.where(hi4 == sub16_h, alive, zero))
                right = []
                for ml in range(4):
                    m = grp * 4 + ml
                    lo = jnp.broadcast_to(lo_all[m:m + 1], (16, GSTEP)).astype(BF)
                    for t16 in range(4):
                        right.append(jnp.where(lo == sub16_f + jnp.array(16 * t16, BF), one, zero))
                acc[grp] += lax.dot_general(
                    jnp.concatenate(left, 0), jnp.concatenate(right, 0),
                    (((1,), (1,)), ((), ())), preferred_element_type=F32)
            return c

        lax.fori_loop(0, SLOTS // GSTEP, step, 0)
        buf = send_sums[g]
        base = pl.multiple_of(u * 24, 8)
        for grp in range(4):
            for pair in range(2):
                q = grp * 2 + pair
                tile = slice(pair * 128, pair * 128 + 128)
                for t in range(2):
                    out = slice(t * 128, t * 128 + 128)
                    cnt = []
                    for m2 in range(2):
                        halves = []
                        for h, here in ((2 * t, m2 == 0), (2 * t + 1, m2 == 1)):
                            at = pair * 64 + h * 16 + m2 * 8
                            row = 128 + h * 4 + pair * 2 + m2
                            s = acc[grp, at:at + 8, tile]
                            n = jnp.broadcast_to(acc[grp, row:row + 1, tile], (8, 128))
                            if not here:
                                s = pltpu.roll(s, 64, 1)
                                n = pltpu.roll(n, 64, 1)
                            halves.append((s, n))
                        buf[q, pl.ds(base + m2 * 8, 8), out] = jnp.where(lane128 < 64, halves[0][0], halves[1][0])
                        cnt.append(jnp.where(lane128 < 64, halves[0][1], halves[1][1]))
                    buf[q, pl.ds(base + 16, 8), out] = jnp.where(row8 == 0, cnt[0], cnt[1])

    def gram_chunk(buf, j, first):
        for i in range(0, j + 1, 2):
            wide = min(2, j + 1 - i)
            right = jnp.concatenate([res[i + k] for k in range(wide)], 1)
            block = lax.dot_general(
                rest[j], right, (((1,), (0,)), ((), ())), preferred_element_type=F32) * (1.0 / (SLOTS * NL * ND))
            for k in range(wide):
                for q in range(ND):
                    buf[q, first + i + k] = block[q * 16:q * 16 + 16, k * CW:(k + 1) * CW].astype(BF)

    def start_dp(a, src, dst):
        def one(s, c):
            q = dp_peer(s)
            pltpu.make_async_remote_copy(
                src_ref=src.at[q], dst_ref=dst.at[dp], send_sem=ar_ssem.at[a, 0], recv_sem=ar_rsem.at[a, 0],
                device_id={"dp": q}, device_id_type=MESH).start()
            return c

        lax.fori_loop(1, ND, one, 0)

    def start_list(a, src, dst):
        def one(s, c):
            p = list_peer(s)
            pltpu.make_async_remote_copy(
                src_ref=src.at[p], dst_ref=dst.at[me], send_sem=ar_ssem.at[a, 1], recv_sem=ar_rsem.at[a, 1],
                device_id={"list": p}, device_id_type=MESH).start()
            return c

        lax.fori_loop(1, NL, one, 0)

    def share_list(a, buf):
        def one(s, c):
            pltpu.make_async_remote_copy(
                src_ref=buf.at[me], dst_ref=buf.at[me], send_sem=ar_ssem.at[a, 2], recv_sem=ar_rsem.at[a, 2],
                device_id={"list": list_peer(s)}, device_id_type=MESH).start()
            return c

        lax.fori_loop(1, NL, one, 0)

    def share_dp(a, buf):
        def one(s, c):
            pltpu.make_async_remote_copy(
                src_ref=buf.at[dp], dst_ref=buf.at[dp], send_sem=ar_ssem.at[a, 3], recv_sem=ar_rsem.at[a, 3],
                device_id={"dp": dp_peer(s)}, device_id_type=MESH).start()
            return c

        lax.fori_loop(1, ND, one, 0)

    recv_sums, ls, lr, ag, ad = (dr0, dr1, dr2), (ls0, ls1, ls2), (lr0, lr1, lr2), (as0, as1, as2), (ad0, ad1, ad2)

    def sums_1(g):
        start_dp(g, send_sums[g], recv_sums[g])

    def sums_2(g):
        src, dst, width = send_sums[g], recv_sums[g], len(GROUPS[g])
        drain(dst.at[pl.ds(0, ND - 1)], ar_rsem.at[g, 0])
        dst[dp] = src[dp]
        total = dst[0]
        for q in range(1, ND):
            total = total + dst[q]
        for u in range(width):
            for p in range(NL):
                ls[g][p, u:u + 1, :] = total[u * 24 + p:u * 24 + p + 1]
                at = u * 24 + 16 + p // 8
                ls[g][p, width + u:width + u + 1, :] = total[at:at + 1]
        start_list(g, ls[g], lr[g])

    def sums_3(g):
        width = len(GROUPS[g])
        drain(lr[g].at[pl.ds(0, NL - 1)], ar_rsem.at[g, 1])
        lr[g][me] = ls[g][me]
        total = lr[g][0]
        for p in range(1, NL):
            total = total + lr[g][p]
        for u in range(width):
            m = GROUPS[g][u] * MC + dp * 2 + me // 8
            old = books[m, pl.ds(lax.rem(me, 8), 1), :]
            ag[g][me, u:u + 1, :] = (total[u:u + 1] + old) / (total[width + u:width + u + 1] + 1.0)
        share_list(g, ag[g])

    def sums_4(g):
        drain(ag[g].at[pl.ds(0, NL - 1)], ar_rsem.at[g, 2])
        for u in range(len(GROUPS[g])):
            for p in range(NL):
                ad[g][dp, u, p:p + 1, :] = ag[g][p, u:u + 1, :]
        share_dp(g, ad[g])

    def sums_5(g):
        drain(ad[g].at[pl.ds(0, ND - 1)], ar_rsem.at[g, 3])

    gs_, gr_, gl_, gm_, gt_, gd_ = (gsa, gsb), (gra, grb), (gla, glb), (gma, gmb), (gta, gtb), (gda, gdb)

    def gram_1(k):
        start_dp(3 + k, gs_[k], gr_[k])

    def gram_2(k):
        drain(gr_[k].at[pl.ds(0, ND - 1)], ar_rsem.at[3 + k, 0])
        blocks = gs_[k].shape[1]

        def one(b, c):
            total = gs_[k][dp, b].astype(F32)
            for s in range(1, ND):
                total = total + gr_[k][dp_peer(s), b].astype(F32)
            gl_[k][b] = total.astype(BF)
            return c

        lax.fori_loop(0, blocks, one, 0)
        for b in range(blocks, NL):
            gl_[k][b] = jnp.zeros((16, CW), BF)
        start_list(3 + k, gl_[k], gm_[k])

    def gram_3(k):
        drain(gm_[k].at[pl.ds(0, NL - 1)], ar_rsem.at[3 + k, 1])
        total = gl_[k][me].astype(F32)
        for s in range(1, NL):
            total = total + gm_[k][list_peer(s)].astype(F32)
        gt_[k][me] = total.astype(BF)
        share_list(3 + k, gt_[k])

    def gram_4(k):
        drain(gt_[k].at[pl.ds(0, NL - 1)], ar_rsem.at[3 + k, 2])
        gd_[k][dp] = gt_[k][:gd_[k].shape[1]]
        share_dp(3 + k, gd_[k])

    def gram_5(k):
        drain(gd_[k].at[pl.ds(0, ND - 1)], ar_rsem.at[3 + k, 3])

    def err_out(j):
        return pltpu.make_async_copy(
            err.at[j], err_hbm.at[:, pl.ds(pl.multiple_of(j * CW, CW), CW)], out_sem.at[0])

    def error_chunk(g, u, j):
        def one(p, c):
            at = pl.ds(pl.multiple_of(p * CAP, CAP), CAP)
            used = lane128 < fill_ref[0, p]
            parts = []
            for m in range(MC):
                code = jnp.broadcast_to(codes[j, m:m + 1, at], (8, 128))
                k = code & 127
                t = ad[g][m // 2, u, (m % 2) * 8:(m % 2) * 8 + 8, :]
                lo = jnp.take_along_axis(t[:, :128], k, axis=1, mode="promise_in_bounds")
                hi = jnp.take_along_axis(t[:, 128:], k, axis=1, mode="promise_in_bounds")
                r = rest[j, m * 8:m * 8 + 8, at].astype(F32)
                parts.append(jnp.where(used, r - jnp.where(code < 128, lo, hi), 0.0))
            err[j, at, :] = jnp.concatenate(parts, 0).astype(BF).T
            return c

        lax.fori_loop(0, NL, one, 0, unroll=4)
        err_out(j).start()

    def book_outs(g):
        return [pltpu.make_async_copy(ad[g].at[:, u], nb_hbm.at[j], out_sem.at[1]) for u, j in enumerate(GROUPS[g])]

    def gram_rows(buf, j, first):
        def one(i, c):
            block = jnp.concatenate([buf[q, first + i].astype(F32) for q in range(ND)], 0)
            jr = pl.ds(pl.multiple_of(j * CW, CW), CW)
            ir = pl.ds(pl.multiple_of(i * CW, CW), CW)
            gram[ir, jr] = block.T
            gram[jr, ir] = block
            return c

        lax.fori_loop(0, j + 1, one, 0)

    def chunk(g, u, j):
        drain(rbuf.at[j, pl.ds(0, NL - 1)], x_rsem.at[j])
        if isinstance(j, int):
            if j + AHEAD < NC:
                send_chunk(j + AHEAD)
        else:
            send_chunk(j + AHEAD)
        residual_chunk(j)
        hist_chunk(g, u, j)

    def gram_early(j):
        gram_chunk(gsa, j, block_of(j, 0))

    chunk(0, 0, 0)
    gram_early(0)
    chunk(0, 1, 1)
    sums_1(0)
    gram_early(1)
    chunk(1, 0, 2)
    gram_early(2)
    sums_2(0)
    chunk(1, 1, 3)
    gram_early(3)
    chunk(1, 2, 4)
    sums_1(1)
    gram_early(4)
    gram_1(0)
    sums_3(0)
    chunk(2, 0, 5)
    sums_1(2)
    sums_2(1)
    gram_2(0)
    gram_chunk(gsb, NC - 1, 0)
    gram_1(1)
    sums_4(0)
    sums_2(2)
    gram_2(1)
    sums_3(1)
    gram_3(0)
    sums_5(0)
    error_chunk(0, 0, 0)
    sums_3(2)
    gram_3(1)
    sums_4(1)
    gram_4(0)
    error_chunk(0, 1, 1)
    sums_4(2)
    gram_4(1)
    sums_5(1)
    error_chunk(1, 0, 2)
    error_chunk(1, 1, 3)
    sums_5(2)
    error_chunk(2, 0, 5)
    error_chunk(1, 2, 4)
    gram_5(0)

    def early_rows(j, c):
        gram_rows(gda, j, block_of(j, 0))
        return c

    lax.fori_loop(0, NC - 1, early_rows, 0)
    gram_5(1)
    gram_rows(gdb, NC - 1, 0)
    gram_out = pltpu.make_async_copy(gram, gram_hbm, out_sem.at[2])
    gram_out.start()
    books_out = [o for g in range(3) for o in book_outs(g)]
    for o in books_out:
        o.start()
    for j in range(NC):
        drain(sbuf.at[j, pl.ds(0, NL - 1)], x_ssem)
    for g in range(3):
        drain(send_sums[g].at[pl.ds(0, ND - 1)], ar_ssem.at[g, 0])
        drain(ls[g].at[pl.ds(0, NL - 1)], ar_ssem.at[g, 1])
        drain(ag[g].at[pl.ds(0, NL - 1)], ar_ssem.at[g, 2])
        drain(ad[g].at[pl.ds(0, ND - 1)], ar_ssem.at[g, 3])
    for k in range(2):
        drain(gs_[k].at[pl.ds(0, ND - 1)], ar_ssem.at[3 + k, 0])
        drain(gl_[k].at[pl.ds(0, NL - 1)], ar_ssem.at[3 + k, 1])
        drain(gt_[k].at[pl.ds(0, NL - 1)], ar_ssem.at[3 + k, 2])
        drain(gd_[k].at[pl.ds(0, ND - 1)], ar_ssem.at[3 + k, 3])
    for j in range(NC):
        err_out(j).wait()
    for o in books_out:
        o.wait()
    gram_out.wait()


def refine(ids, fill, vectors, codes, centroids, codebooks):
    anyspace = pl.BlockSpec(memory_space=pl.ANY)
    V = pltpu.VMEM
    widths = [len(g) for g in GROUPS]
    blocks = (15, 6)
    dma = pltpu.SemaphoreType.DMA
    out_shape = [
        jax.ShapeDtypeStruct((SLOTS, 768), BF),
        jax.ShapeDtypeStruct((NC, ND, 16, 256), F32),
        jax.ShapeDtypeStruct((768, 768), F32),
    ]
    scratch = (
        [
            V((NL, 1, CAP), jnp.int32), pltpu.SMEM((NL, 1, CAP), jnp.int32),
            V((4096, 8, 128), F32), V((4096, 768), BF), V((32, 8, 128), F32),
            V((NC, NL, CAP, CW), BF), V((NC, NL, CAP, CW), BF),
            V((SLOTS, 768), BF), V((NC, MC, SLOTS), jnp.int32), V((96, 8, 256), F32),
            V((NC, SLOTS, CW), BF), V((NC, CW, SLOTS), BF), V((16, SLOTS), BF), V((4, 144, 256), F32),
            V((NC, SLOTS, CW), BF), V((768, 768), F32),
        ]
        + [V((ND, sum_rows(g), 256), F32) for g in range(3)] * 2
        + [V((NL, 2 * w, 256), F32) for w in widths] * 2
        + [V((NL, w, 256), F32) for w in widths]
        + [V((ND, w, NL, 256), F32) for w in widths]
        + [V((ND, b, 16, CW), BF) for b in blocks] * 2
        + [V((NL, 16, CW), BF) for _ in blocks] * 3
        + [V((ND, n, 16, CW), BF) for n in (NL, 6)]
        + [dma((3,)), dma((8,)), dma((3,)), dma, dma, dma, dma, dma((NC,)), dma((5, 4)), dma((5, 4))]
    )
    return pl.pallas_call(
        refine_kernel,
        out_shape=out_shape,
        in_specs=[pl.BlockSpec(memory_space=pltpu.VMEM), pl.BlockSpec(memory_space=pltpu.SMEM)] + [anyspace] * 4,
        out_specs=[anyspace] * 3,
        scratch_shapes=scratch,
        compiler_params=pltpu.CompilerParams(
            collective_id=0, has_side_effects=True, vmem_limit_bytes=60 << 20),
    )(ids, fill, vectors, codes, centroids, codebooks)


def local(vectors, list_ids, codes, fill_counts, centroids, codebooks):
    codes_t = codes.T.reshape(NC, MC, SLOTS)
    err, books, gram = refine(
        list_ids.reshape(NL, 1, CAP), fill_counts, vectors, codes_t, centroids, codebooks)
    return err, books.reshape(96, 8, 256), gram


def solution(mesh):
    in_specs = (
        P(("dp", "list"), None),
        P(("dp", "list")),
        P(("dp", "list"), None),
        P(("dp", "list"), None),
        P("list", None),
        P(),
    )
    out_specs = (P(("dp", "list"), None), P(), P())
    return jax.shard_map(local, mesh=mesh, in_specs=in_specs, out_specs=out_specs, check_vma=False)
```

```python
import functools

import jax
import jax.numpy as jnp
from jax import lax
from jax.experimental import pallas as pl
from jax.experimental.pallas import tpu as pltpu
from jax.sharding import PartitionSpec as P

MESH = pl.DeviceIdType.MESH
F32 = jnp.float32
BF = jnp.bfloat16
NL, ND = 16, 8
CAP = 128
SLOTS = NL * CAP
NC = 6
CW = 128
MC = 16
GROUPS = ((0, 1), (2, 3), (4, 5))
GSTEP = 1024
AHEAD = 2


def sum_rows(g):
    return len(GROUPS[g]) * 24


def block_of(j, i):
    return j * (j + 1) // 2 + i


def drain(ref, sem):
    pltpu.make_async_copy(ref, ref, sem).wait()


def refine_kernel(
    ids_ref, fill_ref, vec_hbm, codes_hbm, cent_hbm, books_hbm,
    err_hbm, nb_hbm, ga_hbm, gb_hbm,
    ids_in, ids_s, table, cbuf, gbuf, sbuf, rbuf, vec, codes, books, res, rest, live, acc, err,
    ds0, ds1, ds2, dr0, dr1, dr2, ls0, ls1, ls2, lr0, lr1, lr2,
    as0, as1, as2, ad0, ad1, ad2,
    gsa, gsb, gra, grb, gla, glb, gma, gmb, gta, gtb, gda, gdb,
    load_sem, cent_sem, out_sem, ids_ssem, ids_rsem, self_sem, x_ssem, x_rsem,
    ar_ssem, ar_rsem,
):
    dp = lax.axis_index("dp")
    me = lax.axis_index("list")
    my_y, my_z = me // 4, me % 4

    def list_peer(s):
        return lax.rem(my_y + s // 4, 4) * 4 + lax.rem(my_z + s % 4, 4)

    def dp_peer(s):
        return lax.rem(dp + s, ND)

    n_cent = cent_sem.shape[0]
    cent_rows = cbuf.shape[0] // n_cent

    def cent_copy(b):
        rows = pl.ds(pl.multiple_of(b * cent_rows, cent_rows), cent_rows)
        return pltpu.make_async_copy(cent_hbm.at[rows], cbuf.at[rows], cent_sem.at[b])

    codes_load = pltpu.make_async_copy(codes_hbm, codes, load_sem.at[0])
    books_load = pltpu.make_async_copy(books_hbm, books, load_sem.at[1])
    vec_load = pltpu.make_async_copy(vec_hbm, vec, load_sem.at[2])
    for b in range(n_cent):
        cent_copy(b).start()
    vec_load.start()
    codes_load.start()
    books_load.start()

    barrier = pltpu.get_barrier_semaphore()

    def greet_list(s, c):
        pl.semaphore_signal(barrier, inc=1, device_id={"list": list_peer(s)}, device_id_type=MESH)
        return c

    def greet_dp(s, c):
        pl.semaphore_signal(barrier, inc=1, device_id={"dp": dp_peer(s)}, device_id_type=MESH)
        return c

    lax.fori_loop(1, NL, greet_list, 0)
    lax.fori_loop(1, ND, greet_dp, 0)

    def send_ids(s, c):
        p = list_peer(s)
        pltpu.make_async_remote_copy(
            src_ref=ids_ref.at[p], dst_ref=ids_in.at[me], send_sem=ids_ssem, recv_sem=ids_rsem,
            device_id={"list": p}, device_id_type=MESH).start()
        return c


    table_rows = table.reshape(4096 * 8, 128)
    gathered_rows = gbuf.reshape(32 * 8, 128)

    def build(b, c):
        cent_copy(b).wait()

        def rows16(r, c):
            row = pl.multiple_of(b * cent_rows + r * 16, 16)
            for j in range(NC):
                v = cbuf[pl.ds(row, 16), j * CW:(j + 1) * CW].astype(F32)
                table_rows[pl.ds(row * 8 + j, 8, stride=8), :] = v[:8]
                table_rows[pl.ds(row * 8 + 64 + j, 8, stride=8), :] = v[8:]
            return c

        return lax.fori_loop(0, cent_rows // 16, rows16, c, unroll=4)

    lax.fori_loop(0, n_cent, build, 0)
    pl.semaphore_wait(barrier, NL + ND - 2)
    lax.fori_loop(1, NL, send_ids, 0)
    ids_in[me] = ids_ref[me]

    lane = lax.broadcasted_iota(jnp.int32, (16, CAP), 1)
    for p in range(NL):
        live[:, p * CAP:(p + 1) * CAP] = (lane < fill_ref[0, p]).astype(F32).astype(BF)

    drain(ids_in.at[pl.ds(0, NL - 1)], ids_rsem)
    drain(ids_in.at[pl.ds(0, NL - 1)], ids_ssem)
    to_smem = pltpu.make_async_copy(ids_in, ids_s, self_sem)
    to_smem.start()
    to_smem.wait()

    def x_copy(j, p):
        return pltpu.make_async_remote_copy(
            src_ref=sbuf.at[j, p], dst_ref=rbuf.at[j, me], send_sem=x_ssem, recv_sem=x_rsem.at[j],
            device_id={"list": p}, device_id_type=MESH)

    def gather(p, dst):
        def rows(r, c):
            for half in range(2):
                for k in range(16):
                    row = ids_s[p, 0, r * 32 + half * 16 + k]
                    gbuf[half * 16 + k] = table[row]
            for half in range(2):
                at = pl.ds(pl.multiple_of(r * 32 + half * 16, 16), 16)
                for j in range(NC):
                    lo = gathered_rows[pl.ds(half * 128 + j, 8, stride=8), :]
                    hi = gathered_rows[pl.ds(half * 128 + 64 + j, 8, stride=8), :]
                    dst[j, p, at, :] = jnp.concatenate([lo, hi], 0).astype(BF)
            return c

        lax.fori_loop(0, CAP // 32, rows, 0)

    def gather_send(s, c):
        p = list_peer(s)
        gather(p, sbuf)
        x_copy(0, p).start()
        return c

    lax.fori_loop(1, NL, gather_send, 0)

    def send_chunk(j):
        def one(s, c):
            x_copy(j, list_peer(s)).start()
            return c

        lax.fori_loop(1, NL, one, 0)

    send_chunk(1)
    gather(me, rbuf)

    vec_load.wait()
    codes_load.wait()
    books_load.wait()

    send_sums = (ds0, ds1, ds2)
    lane128 = lax.broadcasted_iota(jnp.int32, (8, 128), 1)
    row8 = lax.broadcasted_iota(jnp.int32, (8, 128), 0)
    sub16 = lax.broadcasted_iota(jnp.int32, (16, GSTEP), 0)
    sub16_f = sub16.astype(F32).astype(BF)
    sub16_h = (sub16 // 4).astype(F32).astype(BF)

    def residual_chunk(j):
        def one(p, c):
            rows = pl.ds(pl.multiple_of(p * CAP, CAP), CAP)
            v = vec[rows, pl.ds(pl.multiple_of(j * CW, CW), CW)].astype(F32)
            d = v - rbuf[j, p].astype(F32)
            keep = lax.broadcasted_iota(jnp.int32, (CAP, CW), 0) < fill_ref[0, p]
            d = jnp.where(keep, d, 0.0).astype(BF)
            res[j, rows, :] = d
            rest[j, :, pl.ds(pl.multiple_of(p * CAP, CAP), CAP)] = d.T
            return c

        lax.fori_loop(0, NL, one, 0, unroll=4)

    def hist_chunk(g, u, j):
        acc[...] = jnp.zeros_like(acc)

        def step(t, c):
            gs = pl.ds(pl.multiple_of(t * GSTEP, GSTEP), GSTEP)
            code = codes[j, :, gs]
            hi_all = (code >> 6).astype(F32)
            lo_all = (code & 63).astype(F32)
            alive = live[:, gs]
            zero = jnp.zeros((16, GSTEP), BF)
            one = jnp.ones((16, GSTEP), BF)
            for grp in range(4):
                left = []
                for pair in range(2):
                    m = grp * 4 + pair * 2
                    hi2 = jnp.concatenate([
                        jnp.broadcast_to(hi_all[m:m + 1], (8, GSTEP)),
                        jnp.broadcast_to(hi_all[m + 1:m + 2], (8, GSTEP))], 0).astype(BF)
                    r16 = rest[j, m * 8:m * 8 + 16, gs]
                    for h in range(4):
                        left.append(jnp.where(hi2 == jnp.array(h, BF), r16, zero))
                hi4 = hi_all[grp * 4:grp * 4 + 4]
                hi4 = jnp.concatenate([hi4, hi4, hi4, hi4], 0).astype(BF)
                left.append(jnp.where(hi4 == sub16_h, alive, zero))
                right = []
                for ml in range(4):
                    m = grp * 4 + ml
                    lo = jnp.broadcast_to(lo_all[m:m + 1], (16, GSTEP)).astype(BF)
                    for t16 in range(4):
                        right.append(jnp.where(lo == sub16_f + jnp.array(16 * t16, BF), one, zero))
                acc[grp] += lax.dot_general(
                    jnp.concatenate(left, 0), jnp.concatenate(right, 0),
                    (((1,), (1,)), ((), ())), preferred_element_type=F32)
            return c

        lax.fori_loop(0, SLOTS // GSTEP, step, 0)
        buf = send_sums[g]
        base = pl.multiple_of(u * 24, 8)
        for grp in range(4):
            for pair in range(2):
                q = grp * 2 + pair
                tile = slice(pair * 128, pair * 128 + 128)
                for t in range(2):
                    out = slice(t * 128, t * 128 + 128)
                    cnt = []
                    for m2 in range(2):
                        halves = []
                        for h, here in ((2 * t, m2 == 0), (2 * t + 1, m2 == 1)):
                            at = pair * 64 + h * 16 + m2 * 8
                            row = 128 + h * 4 + pair * 2 + m2
                            s = acc[grp, at:at + 8, tile]
                            n = jnp.broadcast_to(acc[grp, row:row + 1, tile], (8, 128))
                            if not here:
                                s = pltpu.roll(s, 64, 1)
                                n = pltpu.roll(n, 64, 1)
                            halves.append((s, n))
                        buf[q, pl.ds(base + m2 * 8, 8), out] = jnp.where(lane128 < 64, halves[0][0], halves[1][0])
                        cnt.append(jnp.where(lane128 < 64, halves[0][1], halves[1][1]))
                    buf[q, pl.ds(base + 16, 8), out] = jnp.where(row8 == 0, cnt[0], cnt[1])

    def gram_chunk(buf, j, first):
        for i in range(0, j + 1, 2):
            wide = min(2, j + 1 - i)
            right = jnp.concatenate([res[i + k] for k in range(wide)], 1)
            block = lax.dot_general(
                rest[j], right, (((1,), (0,)), ((), ())), preferred_element_type=F32) * (1.0 / (SLOTS * NL * ND))
            for k in range(wide):
                for q in range(ND):
                    buf[q, first + i + k] = block[q * 16:q * 16 + 16, k * CW:(k + 1) * CW].astype(BF)

    def start_dp(a, src, dst):
        def one(s, c):
            q = dp_peer(s)
            pltpu.make_async_remote_copy(
                src_ref=src.at[q], dst_ref=dst.at[dp], send_sem=ar_ssem.at[a, 0], recv_sem=ar_rsem.at[a, 0],
                device_id={"dp": q}, device_id_type=MESH).start()
            return c

        lax.fori_loop(1, ND, one, 0)

    def start_list(a, src, dst):
        def one(s, c):
            p = list_peer(s)
            pltpu.make_async_remote_copy(
                src_ref=src.at[p], dst_ref=dst.at[me], send_sem=ar_ssem.at[a, 1], recv_sem=ar_rsem.at[a, 1],
                device_id={"list": p}, device_id_type=MESH).start()
            return c

        lax.fori_loop(1, NL, one, 0)

    def share_list(a, buf):
        def one(s, c):
            pltpu.make_async_remote_copy(
                src_ref=buf.at[me], dst_ref=buf.at[me], send_sem=ar_ssem.at[a, 2], recv_sem=ar_rsem.at[a, 2],
                device_id={"list": list_peer(s)}, device_id_type=MESH).start()
            return c

        lax.fori_loop(1, NL, one, 0)

    def share_dp(a, buf):
        def one(s, c):
            pltpu.make_async_remote_copy(
                src_ref=buf.at[dp], dst_ref=buf.at[dp], send_sem=ar_ssem.at[a, 3], recv_sem=ar_rsem.at[a, 3],
                device_id={"dp": dp_peer(s)}, device_id_type=MESH).start()
            return c

        lax.fori_loop(1, ND, one, 0)

    recv_sums, ls, lr, ag, ad = (dr0, dr1, dr2), (ls0, ls1, ls2), (lr0, lr1, lr2), (as0, as1, as2), (ad0, ad1, ad2)

    def sums_1(g):
        start_dp(g, send_sums[g], recv_sums[g])

    def sums_2(g):
        src, dst, width = send_sums[g], recv_sums[g], len(GROUPS[g])
        drain(dst.at[pl.ds(0, ND - 1)], ar_rsem.at[g, 0])
        dst[dp] = src[dp]
        total = dst[0]
        for q in range(1, ND):
            total = total + dst[q]
        for u in range(width):
            for p in range(NL):
                ls[g][p, u:u + 1, :] = total[u * 24 + p:u * 24 + p + 1]
                at = u * 24 + 16 + p // 8
                ls[g][p, width + u:width + u + 1, :] = total[at:at + 1]
        start_list(g, ls[g], lr[g])

    def sums_3(g):
        width = len(GROUPS[g])
        drain(lr[g].at[pl.ds(0, NL - 1)], ar_rsem.at[g, 1])
        lr[g][me] = ls[g][me]
        total = lr[g][0]
        for p in range(1, NL):
            total = total + lr[g][p]
        for u in range(width):
            m = GROUPS[g][u] * MC + dp * 2 + me // 8
            old = books[m, pl.ds(lax.rem(me, 8), 1), :]
            ag[g][me, u:u + 1, :] = (total[u:u + 1] + old) / (total[width + u:width + u + 1] + 1.0)
        share_list(g, ag[g])

    def sums_4(g):
        drain(ag[g].at[pl.ds(0, NL - 1)], ar_rsem.at[g, 2])
        for u in range(len(GROUPS[g])):
            for p in range(NL):
                ad[g][dp, u, p:p + 1, :] = ag[g][p, u:u + 1, :]
        share_dp(g, ad[g])

    def sums_5(g):
        drain(ad[g].at[pl.ds(0, ND - 1)], ar_rsem.at[g, 3])

    gs_, gr_, gl_, gm_, gt_, gd_ = (gsa, gsb), (gra, grb), (gla, glb), (gma, gmb), (gta, gtb), (gda, gdb)

    def gram_1(k):
        start_dp(3 + k, gs_[k], gr_[k])

    def gram_2(k):
        drain(gr_[k].at[pl.ds(0, ND - 1)], ar_rsem.at[3 + k, 0])
        blocks = gs_[k].shape[1]

        def one(b, c):
            total = gs_[k][dp, b].astype(F32)
            for s in range(1, ND):
                total = total + gr_[k][dp_peer(s), b].astype(F32)
            gl_[k][b] = total.astype(BF)
            return c

        lax.fori_loop(0, blocks, one, 0)
        for b in range(blocks, NL):
            gl_[k][b] = jnp.zeros((16, CW), BF)
        start_list(3 + k, gl_[k], gm_[k])

    def gram_3(k):
        drain(gm_[k].at[pl.ds(0, NL - 1)], ar_rsem.at[3 + k, 1])
        total = gl_[k][me].astype(F32)
        for s in range(1, NL):
            total = total + gm_[k][list_peer(s)].astype(F32)
        mine = pl.ds(pl.multiple_of(dp * 16, 16), 16)
        gt_[k][mine, :] = total.astype(BF)

        def one(s, c):
            pltpu.make_async_remote_copy(
                src_ref=gt_[k].at[mine], dst_ref=gt_[k].at[mine], send_sem=ar_ssem.at[3 + k, 2],
                recv_sem=ar_rsem.at[3 + k, 2], device_id={"dp": dp_peer(s)}, device_id_type=MESH).start()
            return c

        lax.fori_loop(1, ND, one, 0)

    def with_block(k, yes, no=None):
        owners = gd_[k].shape[0]
        if owners == NL:
            yes()
        else:
            pl.when(me < owners)(yes)
            if no is not None:
                pl.when(me >= owners)(no)

    def gram_4(k):
        drain(gt_[k].at[pl.ds(0, 112)], ar_rsem.at[3 + k, 2])

        def send():
            gd_[k][me] = gt_[k][...]

            def one(s, c):
                pltpu.make_async_remote_copy(
                    src_ref=gt_[k], dst_ref=gd_[k].at[me], send_sem=ar_ssem.at[3 + k, 3],
                    recv_sem=ar_rsem.at[3 + k, 3], device_id={"list": list_peer(s)}, device_id_type=MESH).start()
                return c

            lax.fori_loop(1, NL, one, 0)

        with_block(k, send)

    def gram_5(k):
        owners = gd_[k].shape[0]
        with_block(
            k,
            lambda: drain(gd_[k].at[pl.ds(0, owners - 1)], ar_rsem.at[3 + k, 3]),
            lambda: drain(gd_[k], ar_rsem.at[3 + k, 3]))

    def err_out(j):
        return pltpu.make_async_copy(
            err.at[j], err_hbm.at[:, pl.ds(pl.multiple_of(j * CW, CW), CW)], out_sem.at[0])

    def error_chunk(g, u, j):
        def one(p, c):
            at = pl.ds(pl.multiple_of(p * CAP, CAP), CAP)
            used = lane128 < fill_ref[0, p]
            parts = []
            for m in range(MC):
                code = jnp.broadcast_to(codes[j, m:m + 1, at], (8, 128))
                k = code & 127
                t = ad[g][m // 2, u, (m % 2) * 8:(m % 2) * 8 + 8, :]
                lo = jnp.take_along_axis(t[:, :128], k, axis=1, mode="promise_in_bounds")
                hi = jnp.take_along_axis(t[:, 128:], k, axis=1, mode="promise_in_bounds")
                r = rest[j, m * 8:m * 8 + 8, at].astype(F32)
                parts.append(jnp.where(used, r - jnp.where(code < 128, lo, hi), 0.0))
            err[j, at, :] = jnp.concatenate(parts, 0).astype(BF).T
            return c

        lax.fori_loop(0, NL, one, 0, unroll=4)
        err_out(j).start()

    def book_outs(g):
        return [pltpu.make_async_copy(ad[g].at[:, u], nb_hbm.at[j], out_sem.at[1]) for u, j in enumerate(GROUPS[g])]

    def chunk(g, u, j, arrived=None):
        drain(rbuf.at[j, pl.ds(0, NL - 1)], x_rsem.at[j])
        if arrived is not None:
            arrived(0)
        if j + AHEAD < NC:
            send_chunk(j + AHEAD)
        residual_chunk(j)
        hist_chunk(g, u, j)

    def gram_early(j):
        gram_chunk(gsa, j, block_of(j, 0))

    chunk(0, 0, 0)
    gram_early(0)
    chunk(0, 1, 1)
    sums_1(0)
    gram_early(1)
    chunk(1, 0, 2)
    gram_early(2)
    chunk(1, 1, 3, sums_2)
    sums_1(1)
    gram_early(3)
    chunk(2, 0, 4, sums_3)
    gram_early(4)
    gram_1(0)
    chunk(2, 1, 5, lambda g: (sums_4(0), sums_2(1)))
    sums_1(2)
    gram_chunk(gsb, NC - 1, 0)
    gram_1(1)
    gram_2(0)
    sums_3(1)
    sums_2(2)
    gram_2(1)
    sums_5(0)
    error_chunk(0, 0, 0)
    sums_4(1)
    sums_3(2)
    gram_3(0)
    gram_3(1)
    error_chunk(0, 1, 1)
    sums_4(2)
    gram_4(1)
    gram_4(0)
    sums_5(1)
    error_chunk(1, 0, 2)
    error_chunk(1, 1, 3)
    sums_5(2)
    error_chunk(2, 0, 4)
    error_chunk(2, 1, 5)
    gram_5(1)
    gram_5(0)
    outs = [o for g in range(3) for o in book_outs(g)]
    outs += [pltpu.make_async_copy(gda, ga_hbm, out_sem.at[2]), pltpu.make_async_copy(gdb, gb_hbm, out_sem.at[2])]
    for o in outs:
        o.start()
    for j in range(NC):
        drain(sbuf.at[j, pl.ds(0, NL - 1)], x_ssem)
    for g in range(3):
        drain(send_sums[g].at[pl.ds(0, ND - 1)], ar_ssem.at[g, 0])
        drain(ls[g].at[pl.ds(0, NL - 1)], ar_ssem.at[g, 1])
        drain(ag[g].at[pl.ds(0, NL - 1)], ar_ssem.at[g, 2])
        drain(ad[g].at[pl.ds(0, ND - 1)], ar_ssem.at[g, 3])
    for k in range(2):
        drain(gs_[k].at[pl.ds(0, ND - 1)], ar_ssem.at[3 + k, 0])
        drain(gl_[k].at[pl.ds(0, NL - 1)], ar_ssem.at[3 + k, 1])
        drain(gt_[k].at[pl.ds(0, 112)], ar_ssem.at[3 + k, 2])
        with_block(k, lambda: drain(gda.at[pl.ds(0, NL - 1)], ar_ssem.at[3 + k, 3]))
    for j in range(NC):
        err_out(j).wait()
    for o in outs:
        o.wait()


def refine(ids, fill, vectors, codes, centroids, codebooks):
    anyspace = pl.BlockSpec(memory_space=pl.ANY)
    V = pltpu.VMEM
    widths = [len(g) for g in GROUPS]
    blocks = (15, 6)
    dma = pltpu.SemaphoreType.DMA
    out_shape = [
        jax.ShapeDtypeStruct((SLOTS, 768), BF),
        jax.ShapeDtypeStruct((NC, ND, 16, 256), F32),
        jax.ShapeDtypeStruct((NL, CW, CW), BF),
        jax.ShapeDtypeStruct((6, CW, CW), BF),
    ]
    scratch = (
        [
            V((NL, 1, CAP), jnp.int32), pltpu.SMEM((NL, 1, CAP), jnp.int32),
            V((4096, 8, 128), F32), V((4096, 768), BF), V((32, 8, 128), F32),
            V((NC, NL, CAP, CW), BF), V((NC, NL, CAP, CW), BF),
            V((SLOTS, 768), BF), V((NC, MC, SLOTS), jnp.int32), V((96, 8, 256), F32),
            V((NC, SLOTS, CW), BF), V((NC, CW, SLOTS), BF), V((16, SLOTS), BF), V((4, 144, 256), F32),
            V((NC, SLOTS, CW), BF),
        ]
        + [V((ND, sum_rows(g), 256), F32) for g in range(3)] * 2
        + [V((NL, 2 * w, 256), F32) for w in widths] * 2
        + [V((NL, w, 256), F32) for w in widths]
        + [V((ND, w, NL, 256), F32) for w in widths]
        + [V((ND, b, 16, CW), BF) for b in blocks] * 2
        + [V((NL, 16, CW), BF) for _ in blocks] * 2
        + [V((CW, CW), BF) for _ in blocks]
        + [V((n, CW, CW), BF) for n in (NL, 6)]
        + [dma((3,)), dma((8,)), dma((3,)), dma, dma, dma, dma, dma((NC,)), dma((5, 4)), dma((5, 4))]
    )
    return pl.pallas_call(
        refine_kernel,
        out_shape=out_shape,
        in_specs=[pl.BlockSpec(memory_space=pltpu.VMEM), pl.BlockSpec(memory_space=pltpu.SMEM)] + [anyspace] * 4,
        out_specs=[anyspace] * 4,
        scratch_shapes=scratch,
        compiler_params=pltpu.CompilerParams(
            collective_id=0, has_side_effects=True, vmem_limit_bytes=60 << 20),
    )(ids, fill, vectors, codes, centroids, codebooks)


def finish_kernel(
    err_in, books_in, ga_in, gb_in, err_out, books_out, gram_out, err, books, ga, gb, gram, in_sem, out_sem, gram_sem,
):
    parts = in_sem.shape[0] - 1
    rows = err_in.shape[0] // parts

    def pair(src, held, dst, i):
        return pltpu.make_async_copy(src, held, in_sem.at[i]), pltpu.make_async_copy(held, dst, out_sem.at[i])

    moves = []
    for i in range(parts):
        at = pl.ds(i * rows, rows)
        moves.append(pair(err_in.at[at], err.at[at], err_out.at[at], i))
    moves.append(pair(books_in, books, books_out, parts))
    loads = [pltpu.make_async_copy(ga_in, ga, gram_sem.at[0]), pltpu.make_async_copy(gb_in, gb, gram_sem.at[1])]
    for c in loads:
        c.start()
    for first, _ in moves:
        first.start()
    for c in loads:
        c.wait()
    for j in range(NC):
        for i in range(j + 1):
            block = (ga[block_of(j, i)] if j < NC - 1 else gb[i]).astype(F32)
            jr, ir = slice(j * CW, (j + 1) * CW), slice(i * CW, (i + 1) * CW)
            gram[jr, ir] = block
            if i < j:
                gram[ir, jr] = block.T
    out = pltpu.make_async_copy(gram, gram_out, gram_sem.at[0])
    out.start()
    for first, second in moves:
        first.wait()
        second.start()
    for _, second in moves:
        second.wait()
    out.wait()


def finish(err, books, ga, gb):
    anyspace = pl.BlockSpec(memory_space=pl.ANY)
    dma = pltpu.SemaphoreType.DMA
    return pl.pallas_call(
        finish_kernel,
        out_shape=[
            jax.ShapeDtypeStruct(err.shape, BF),
            jax.ShapeDtypeStruct(books.shape, F32),
            jax.ShapeDtypeStruct((768, 768), F32),
        ],
        in_specs=[anyspace] * 4,
        out_specs=[anyspace] * 3,
        scratch_shapes=[
            pltpu.VMEM(err.shape, BF), pltpu.VMEM(books.shape, F32),
            pltpu.VMEM(ga.shape, BF), pltpu.VMEM(gb.shape, BF), pltpu.VMEM((768, 768), F32),
            dma((9,)), dma((9,)), dma((2,)),
        ],
        compiler_params=pltpu.CompilerParams(vmem_limit_bytes=60 << 20),
    )(err, books, ga, gb)


def local(vectors, list_ids, codes, fill_counts, centroids, codebooks):
    codes_t = codes.T.reshape(NC, MC, SLOTS)
    err, books, ga, gb = refine(
        list_ids.reshape(NL, 1, CAP), fill_counts, vectors, codes_t, centroids, codebooks)
    err, books, gram = finish(err, books, ga, gb)
    return err, books.reshape(96, 8, 256), gram


def solution(mesh):
    in_specs = (
        P(("dp", "list"), None),
        P(("dp", "list")),
        P(("dp", "list"), None),
        P(("dp", "list"), None),
        P("list", None),
        P(),
    )
    out_specs = (P(("dp", "list"), None), P(), P())
    return jax.shard_map(local, mesh=mesh, in_specs=in_specs, out_specs=out_specs, check_vma=False)
```

```python
import functools

import jax
import jax.numpy as jnp
from jax import lax
from jax.experimental import pallas as pl
from jax.experimental.pallas import tpu as pltpu
from jax.sharding import PartitionSpec as P

MESH = pl.DeviceIdType.MESH
F32 = jnp.float32
BF = jnp.bfloat16
NL, ND = 16, 8
CAP = 128
SLOTS = NL * CAP
NC = 6
CW = 128
MC = 16
GROUPS = ((0, 1), (2, 3), (4, 5))
GSTEP = 1024
AHEAD = 2


def sum_rows(g):
    return len(GROUPS[g]) * 24


def block_of(j, i):
    return j * (j + 1) // 2 + i


def drain(ref, sem):
    pltpu.make_async_copy(ref, ref, sem).wait()


def refine_kernel(
    ids_ref, fill_ref, vec_hbm, codes_hbm, cent_hbm, books_hbm,
    err_hbm, nb_hbm, ga_hbm, gb_hbm,
    ids_in, ids_s, table, cbuf, gbuf, sbuf, rbuf, vec, codes, books, res, rest, live, acc, err,
    ds0, ds1, ds2, dr0, dr1, dr2, ls0, ls1, ls2, lr0, lr1, lr2,
    as0, as1, as2, ad0, ad1, ad2,
    gsa, gsb, gra, grb, gla, glb, gma, gmb, gta, gtb, gda, gdb,
    load_sem, cent_sem, out_sem, ids_ssem, ids_rsem, self_sem, x_ssem, x_rsem,
    ar_ssem, ar_rsem,
):
    dp = lax.axis_index("dp")
    me = lax.axis_index("list")
    my_y, my_z = me // 4, me % 4

    def list_peer(s):
        return lax.rem(my_y + s // 4, 4) * 4 + lax.rem(my_z + s % 4, 4)

    def dp_peer(s):
        return lax.rem(dp + s, ND)

    n_cent = cent_sem.shape[0]
    cent_rows = cbuf.shape[0] // n_cent

    def cent_copy(b):
        rows = pl.ds(pl.multiple_of(b * cent_rows, cent_rows), cent_rows)
        return pltpu.make_async_copy(cent_hbm.at[rows], cbuf.at[rows], cent_sem.at[b])

    codes_load = pltpu.make_async_copy(codes_hbm, codes, load_sem.at[0])
    books_load = pltpu.make_async_copy(books_hbm, books, load_sem.at[1])
    vec_load = pltpu.make_async_copy(vec_hbm, vec, load_sem.at[2])
    for b in range(n_cent):
        cent_copy(b).start()
    vec_load.start()
    codes_load.start()
    books_load.start()

    barrier = pltpu.get_barrier_semaphore()

    def greet_list(s, c):
        pl.semaphore_signal(barrier, inc=1, device_id={"list": list_peer(s)}, device_id_type=MESH)
        return c

    def greet_dp(s, c):
        pl.semaphore_signal(barrier, inc=1, device_id={"dp": dp_peer(s)}, device_id_type=MESH)
        return c

    lax.fori_loop(1, NL, greet_list, 0)
    lax.fori_loop(1, ND, greet_dp, 0)

    def send_ids(s, c):
        p = list_peer(s)
        pltpu.make_async_remote_copy(
            src_ref=ids_ref.at[p], dst_ref=ids_in.at[me], send_sem=ids_ssem, recv_sem=ids_rsem,
            device_id={"list": p}, device_id_type=MESH).start()
        return c


    table_rows = table.reshape(4096 * 8, 128)
    gathered_rows = gbuf.reshape(32 * 8, 128)

    def build(b, c):
        cent_copy(b).wait()

        def rows16(r, c):
            row = pl.multiple_of(b * cent_rows + r * 16, 16)
            for j in range(NC):
                v = cbuf[pl.ds(row, 16), j * CW:(j + 1) * CW].astype(F32)
                table_rows[pl.ds(row * 8 + j, 8, stride=8), :] = v[:8]
                table_rows[pl.ds(row * 8 + 64 + j, 8, stride=8), :] = v[8:]
            return c

        return lax.fori_loop(0, cent_rows // 16, rows16, c, unroll=4)

    lax.fori_loop(0, n_cent, build, 0)
    pl.semaphore_wait(barrier, NL + ND - 2)
    lax.fori_loop(1, NL, send_ids, 0)
    ids_in[me] = ids_ref[me]

    lane = lax.broadcasted_iota(jnp.int32, (16, CAP), 1)
    for p in range(NL):
        live[:, p * CAP:(p + 1) * CAP] = (lane < fill_ref[0, p]).astype(F32).astype(BF)

    drain(ids_in.at[pl.ds(0, NL - 1)], ids_rsem)
    drain(ids_in.at[pl.ds(0, NL - 1)], ids_ssem)
    to_smem = pltpu.make_async_copy(ids_in, ids_s, self_sem)
    to_smem.start()
    to_smem.wait()

    def x_copy(j, p):
        return pltpu.make_async_remote_copy(
            src_ref=sbuf.at[j, p], dst_ref=rbuf.at[j, me], send_sem=x_ssem, recv_sem=x_rsem.at[j],
            device_id={"list": p}, device_id_type=MESH)

    def gather(p, dst):
        def rows(r, c):
            for half in range(2):
                for k in range(16):
                    row = ids_s[p, 0, r * 32 + half * 16 + k]
                    gbuf[half * 16 + k] = table[row]
            for half in range(2):
                at = pl.ds(pl.multiple_of(r * 32 + half * 16, 16), 16)
                for j in range(NC):
                    lo = gathered_rows[pl.ds(half * 128 + j, 8, stride=8), :]
                    hi = gathered_rows[pl.ds(half * 128 + 64 + j, 8, stride=8), :]
                    dst[j, p, at, :] = jnp.concatenate([lo, hi], 0).astype(BF)
            return c

        lax.fori_loop(0, CAP // 32, rows, 0)

    def gather_send(s, c):
        p = list_peer(s)
        gather(p, sbuf)
        x_copy(0, p).start()
        return c

    lax.fori_loop(1, NL, gather_send, 0)

    def send_chunk(j):
        def one(s, c):
            x_copy(j, list_peer(s)).start()
            return c

        lax.fori_loop(1, NL, one, 0)

    send_chunk(1)
    gather(me, rbuf)

    vec_load.wait()
    codes_load.wait()
    books_load.wait()

    send_sums = (ds0, ds1, ds2)
    lane128 = lax.broadcasted_iota(jnp.int32, (8, 128), 1)
    row8 = lax.broadcasted_iota(jnp.int32, (8, 128), 0)
    sub16 = lax.broadcasted_iota(jnp.int32, (16, GSTEP), 0)
    sub16_f = sub16.astype(F32).astype(BF)
    sub16_h = (sub16 // 4).astype(F32).astype(BF)

    def residual_chunk(j):
        def one(p, c):
            rows = pl.ds(pl.multiple_of(p * CAP, CAP), CAP)
            v = vec[rows, pl.ds(pl.multiple_of(j * CW, CW), CW)].astype(F32)
            d = v - rbuf[j, p].astype(F32)
            keep = lax.broadcasted_iota(jnp.int32, (CAP, CW), 0) < fill_ref[0, p]
            d = jnp.where(keep, d, 0.0).astype(BF)
            res[j, rows, :] = d
            rest[j, :, pl.ds(pl.multiple_of(p * CAP, CAP), CAP)] = d.T
            return c

        lax.fori_loop(0, NL, one, 0, unroll=4)

    def hist_chunk(g, u, j):
        acc[...] = jnp.zeros_like(acc)

        def step(t, c):
            gs = pl.ds(pl.multiple_of(t * GSTEP, GSTEP), GSTEP)
            code = codes[j, :, gs]
            hi_all = (code >> 6).astype(F32)
            lo_all = (code & 63).astype(F32)
            alive = live[:, gs]
            zero = jnp.zeros((16, GSTEP), BF)
            one = jnp.ones((16, GSTEP), BF)
            for grp in range(4):
                left = []
                for pair in range(2):
                    m = grp * 4 + pair * 2
                    hi2 = jnp.concatenate([
                        jnp.broadcast_to(hi_all[m:m + 1], (8, GSTEP)),
                        jnp.broadcast_to(hi_all[m + 1:m + 2], (8, GSTEP))], 0).astype(BF)
                    r16 = rest[j, m * 8:m * 8 + 16, gs]
                    for h in range(4):
                        left.append(jnp.where(hi2 == jnp.array(h, BF), r16, zero))
                hi4 = hi_all[grp * 4:grp * 4 + 4]
                hi4 = jnp.concatenate([hi4, hi4, hi4, hi4], 0).astype(BF)
                left.append(jnp.where(hi4 == sub16_h, alive, zero))
                right = []
                for ml in range(4):
                    m = grp * 4 + ml
                    lo = jnp.broadcast_to(lo_all[m:m + 1], (16, GSTEP)).astype(BF)
                    for t16 in range(4):
                        right.append(jnp.where(lo == sub16_f + jnp.array(16 * t16, BF), one, zero))
                acc[grp] += lax.dot_general(
                    jnp.concatenate(left, 0), jnp.concatenate(right, 0),
                    (((1,), (1,)), ((), ())), preferred_element_type=F32)
            return c

        lax.fori_loop(0, SLOTS // GSTEP, step, 0)
        buf = send_sums[g]
        base = pl.multiple_of(u * 24, 8)
        for grp in range(4):
            for pair in range(2):
                q = grp * 2 + pair
                tile = slice(pair * 128, pair * 128 + 128)
                for t in range(2):
                    out = slice(t * 128, t * 128 + 128)
                    cnt = []
                    for m2 in range(2):
                        halves = []
                        for h, here in ((2 * t, m2 == 0), (2 * t + 1, m2 == 1)):
                            at = pair * 64 + h * 16 + m2 * 8
                            row = 128 + h * 4 + pair * 2 + m2
                            s = acc[grp, at:at + 8, tile]
                            n = jnp.broadcast_to(acc[grp, row:row + 1, tile], (8, 128))
                            if not here:
                                s = pltpu.roll(s, 64, 1)
                                n = pltpu.roll(n, 64, 1)
                            halves.append((s, n))
                        buf[q, pl.ds(base + m2 * 8, 8), out] = jnp.where(lane128 < 64, halves[0][0], halves[1][0])
                        cnt.append(jnp.where(lane128 < 64, halves[0][1], halves[1][1]))
                    buf[q, pl.ds(base + 16, 8), out] = jnp.where(row8 == 0, cnt[0], cnt[1])

    def gram_chunk(buf, j, first):
        for i in range(0, j + 1, 2):
            wide = min(2, j + 1 - i)
            right = jnp.concatenate([res[i + k] for k in range(wide)], 1)
            block = lax.dot_general(
                rest[j], right, (((1,), (0,)), ((), ())), preferred_element_type=F32) * (1.0 / (SLOTS * NL * ND))
            for k in range(wide):
                for q in range(ND):
                    buf[q, first + i + k] = block[q * 16:q * 16 + 16, k * CW:(k + 1) * CW].astype(BF)

    def start_dp(a, src, dst, part):
        def one(s, c):
            q = dp_peer(s)
            pltpu.make_async_remote_copy(
                src_ref=src.at[q, part], dst_ref=dst.at[dp, part], send_sem=ar_ssem.at[a, 0],
                recv_sem=ar_rsem.at[a, 0], device_id={"dp": q}, device_id_type=MESH).start()
            return c

        lax.fori_loop(1, ND, one, 0)

    def start_list(a, src, dst):
        def one(s, c):
            p = list_peer(s)
            pltpu.make_async_remote_copy(
                src_ref=src.at[p], dst_ref=dst.at[me], send_sem=ar_ssem.at[a, 1], recv_sem=ar_rsem.at[a, 1],
                device_id={"list": p}, device_id_type=MESH).start()
            return c

        lax.fori_loop(1, NL, one, 0)

    def share_list(a, buf):
        def one(s, c):
            pltpu.make_async_remote_copy(
                src_ref=buf.at[me], dst_ref=buf.at[me], send_sem=ar_ssem.at[a, 2], recv_sem=ar_rsem.at[a, 2],
                device_id={"list": list_peer(s)}, device_id_type=MESH).start()
            return c

        lax.fori_loop(1, NL, one, 0)

    def share_dp(a, buf):
        def one(s, c):
            pltpu.make_async_remote_copy(
                src_ref=buf.at[dp], dst_ref=buf.at[dp], send_sem=ar_ssem.at[a, 3], recv_sem=ar_rsem.at[a, 3],
                device_id={"dp": dp_peer(s)}, device_id_type=MESH).start()
            return c

        lax.fori_loop(1, ND, one, 0)

    recv_sums, ls, lr, ag, ad = (dr0, dr1, dr2), (ls0, ls1, ls2), (lr0, lr1, lr2), (as0, as1, as2), (ad0, ad1, ad2)

    def sums_1(g, u):
        start_dp(g, send_sums[g], recv_sums[g], pl.ds(u * 24, 24))

    def sums_2(g):
        src, dst, width = send_sums[g], recv_sums[g], len(GROUPS[g])
        drain(dst.at[pl.ds(0, ND - 1)], ar_rsem.at[g, 0])
        dst[dp] = src[dp]
        total = dst[0]
        for q in range(1, ND):
            total = total + dst[q]
        for u in range(width):
            for p in range(NL):
                ls[g][p, u:u + 1, :] = total[u * 24 + p:u * 24 + p + 1]
                at = u * 24 + 16 + p // 8
                ls[g][p, width + u:width + u + 1, :] = total[at:at + 1]
        start_list(g, ls[g], lr[g])

    def sums_3(g):
        width = len(GROUPS[g])
        drain(lr[g].at[pl.ds(0, NL - 1)], ar_rsem.at[g, 1])
        lr[g][me] = ls[g][me]
        total = lr[g][0]
        for p in range(1, NL):
            total = total + lr[g][p]
        for u in range(width):
            m = GROUPS[g][u] * MC + dp * 2 + me // 8
            old = books[m, pl.ds(lax.rem(me, 8), 1), :]
            ag[g][me, u:u + 1, :] = (total[u:u + 1] + old) / (total[width + u:width + u + 1] + 1.0)
        share_list(g, ag[g])

    def sums_4(g):
        drain(ag[g].at[pl.ds(0, NL - 1)], ar_rsem.at[g, 2])
        for u in range(len(GROUPS[g])):
            for p in range(NL):
                ad[g][dp, u, p:p + 1, :] = ag[g][p, u:u + 1, :]
        share_dp(g, ad[g])

    def sums_5(g):
        drain(ad[g].at[pl.ds(0, ND - 1)], ar_rsem.at[g, 3])

    gs_, gr_, gl_, gm_, gt_, gd_ = (gsa, gsb), (gra, grb), (gla, glb), (gma, gmb), (gta, gtb), (gda, gdb)

    def gram_1(k, first, count):
        start_dp(3 + k, gs_[k], gr_[k], pl.ds(first, count))

    def gram_2(k):
        drain(gr_[k].at[pl.ds(0, ND - 1)], ar_rsem.at[3 + k, 0])
        blocks = gs_[k].shape[1]

        def one(b, c):
            total = gs_[k][dp, b].astype(F32)
            for s in range(1, ND):
                total = total + gr_[k][dp_peer(s), b].astype(F32)
            gl_[k][b] = total.astype(BF)
            return c

        lax.fori_loop(0, blocks, one, 0)
        for b in range(blocks, NL):
            gl_[k][b] = jnp.zeros((16, CW), BF)
        start_list(3 + k, gl_[k], gm_[k])

    def gram_3(k):
        drain(gm_[k].at[pl.ds(0, NL - 1)], ar_rsem.at[3 + k, 1])
        total = gl_[k][me].astype(F32)
        for s in range(1, NL):
            total = total + gm_[k][list_peer(s)].astype(F32)
        mine = pl.ds(pl.multiple_of(dp * 16, 16), 16)
        gt_[k][mine, :] = total.astype(BF)

        def one(s, c):
            pltpu.make_async_remote_copy(
                src_ref=gt_[k].at[mine], dst_ref=gt_[k].at[mine], send_sem=ar_ssem.at[3 + k, 2],
                recv_sem=ar_rsem.at[3 + k, 2], device_id={"dp": dp_peer(s)}, device_id_type=MESH).start()
            return c

        lax.fori_loop(1, ND, one, 0)

    def with_block(k, yes, no=None):
        owners = gd_[k].shape[0]
        if owners == NL:
            yes()
        else:
            pl.when(me < owners)(yes)
            if no is not None:
                pl.when(me >= owners)(no)

    def gram_4(k):
        drain(gt_[k].at[pl.ds(0, 112)], ar_rsem.at[3 + k, 2])

        def send():
            gd_[k][me] = gt_[k][...]

            def one(s, c):
                pltpu.make_async_remote_copy(
                    src_ref=gt_[k], dst_ref=gd_[k].at[me], send_sem=ar_ssem.at[3 + k, 3],
                    recv_sem=ar_rsem.at[3 + k, 3], device_id={"list": list_peer(s)}, device_id_type=MESH).start()
                return c

            lax.fori_loop(1, NL, one, 0)

        with_block(k, send)

    def gram_5(k):
        owners = gd_[k].shape[0]
        with_block(
            k,
            lambda: drain(gd_[k].at[pl.ds(0, owners - 1)], ar_rsem.at[3 + k, 3]),
            lambda: drain(gd_[k], ar_rsem.at[3 + k, 3]))

    def err_out(j):
        return pltpu.make_async_copy(
            err.at[j], err_hbm.at[:, pl.ds(pl.multiple_of(j * CW, CW), CW)], out_sem.at[0])

    def error_chunk(g, u, j):
        def one(p, c):
            at = pl.ds(pl.multiple_of(p * CAP, CAP), CAP)
            used = lane128 < fill_ref[0, p]
            parts = []
            for m in range(MC):
                code = jnp.broadcast_to(codes[j, m:m + 1, at], (8, 128))
                k = code & 127
                t = ad[g][m // 2, u, (m % 2) * 8:(m % 2) * 8 + 8, :]
                lo = jnp.take_along_axis(t[:, :128], k, axis=1, mode="promise_in_bounds")
                hi = jnp.take_along_axis(t[:, 128:], k, axis=1, mode="promise_in_bounds")
                r = rest[j, m * 8:m * 8 + 8, at].astype(F32)
                parts.append(jnp.where(used, r - jnp.where(code < 128, lo, hi), 0.0))
            err[j, at, :] = jnp.concatenate(parts, 0).astype(BF).T
            return c

        lax.fori_loop(0, NL, one, 0, unroll=4)
        err_out(j).start()

    def book_outs(g):
        return [pltpu.make_async_copy(ad[g].at[:, u], nb_hbm.at[j], out_sem.at[1]) for u, j in enumerate(GROUPS[g])]

    def chunk(g, u, j, arrived=None):
        drain(rbuf.at[j, pl.ds(0, NL - 1)], x_rsem.at[j])
        if arrived is not None:
            arrived(0)
        if j + AHEAD < NC:
            send_chunk(j + AHEAD)
        residual_chunk(j)
        hist_chunk(g, u, j)

    def gram_early(j):
        gram_chunk(gsa, j, block_of(j, 0))
        gram_1(0, block_of(j, 0), j + 1)

    chunk(0, 0, 0)
    sums_1(0, 0)
    gram_early(0)
    chunk(0, 1, 1)
    sums_1(0, 1)
    gram_early(1)
    chunk(1, 0, 2)
    sums_1(1, 0)
    gram_early(2)
    chunk(1, 1, 3, sums_2)
    sums_1(1, 1)
    gram_early(3)
    chunk(2, 0, 4, sums_3)
    sums_1(2, 0)
    gram_early(4)
    chunk(2, 1, 5, lambda g: (sums_4(0), sums_2(1)))
    sums_1(2, 1)
    gram_chunk(gsb, NC - 1, 0)
    gram_1(1, 0, NC)
    gram_2(0)
    sums_3(1)
    sums_2(2)
    gram_2(1)
    sums_5(0)
    error_chunk(0, 0, 0)
    sums_4(1)
    sums_3(2)
    gram_3(0)
    gram_3(1)
    error_chunk(0, 1, 1)
    sums_4(2)
    gram_4(1)
    gram_4(0)
    sums_5(1)
    error_chunk(1, 0, 2)
    error_chunk(1, 1, 3)
    sums_5(2)
    error_chunk(2, 0, 4)
    error_chunk(2, 1, 5)
    gram_5(1)
    gram_5(0)
    outs = [o for g in range(3) for o in book_outs(g)]
    outs += [pltpu.make_async_copy(gda, ga_hbm, out_sem.at[2]), pltpu.make_async_copy(gdb, gb_hbm, out_sem.at[2])]
    for o in outs:
        o.start()
    for j in range(NC):
        drain(sbuf.at[j, pl.ds(0, NL - 1)], x_ssem)
    for g in range(3):
        drain(send_sums[g].at[pl.ds(0, ND - 1)], ar_ssem.at[g, 0])
        drain(ls[g].at[pl.ds(0, NL - 1)], ar_ssem.at[g, 1])
        drain(ag[g].at[pl.ds(0, NL - 1)], ar_ssem.at[g, 2])
        drain(ad[g].at[pl.ds(0, ND - 1)], ar_ssem.at[g, 3])
    for k in range(2):
        drain(gs_[k].at[pl.ds(0, ND - 1)], ar_ssem.at[3 + k, 0])
        drain(gl_[k].at[pl.ds(0, NL - 1)], ar_ssem.at[3 + k, 1])
        drain(gt_[k].at[pl.ds(0, 112)], ar_ssem.at[3 + k, 2])
        with_block(k, lambda: drain(gda.at[pl.ds(0, NL - 1)], ar_ssem.at[3 + k, 3]))
    for j in range(NC):
        err_out(j).wait()
    for o in outs:
        o.wait()


def refine(ids, fill, vectors, codes, centroids, codebooks):
    anyspace = pl.BlockSpec(memory_space=pl.ANY)
    V = pltpu.VMEM
    widths = [len(g) for g in GROUPS]
    blocks = (15, 6)
    dma = pltpu.SemaphoreType.DMA
    out_shape = [
        jax.ShapeDtypeStruct((SLOTS, 768), BF),
        jax.ShapeDtypeStruct((NC, ND, 16, 256), F32),
        jax.ShapeDtypeStruct((NL, CW, CW), BF),
        jax.ShapeDtypeStruct((6, CW, CW), BF),
    ]
    scratch = (
        [
            V((NL, 1, CAP), jnp.int32), pltpu.SMEM((NL, 1, CAP), jnp.int32),
            V((4096, 8, 128), F32), V((4096, 768), BF), V((32, 8, 128), F32),
            V((NC, NL, CAP, CW), BF), V((NC, NL, CAP, CW), BF),
            V((SLOTS, 768), BF), V((NC, MC, SLOTS), jnp.int32), V((96, 8, 256), F32),
            V((NC, SLOTS, CW), BF), V((NC, CW, SLOTS), BF), V((16, SLOTS), BF), V((4, 144, 256), F32),
            V((NC, SLOTS, CW), BF),
        ]
        + [V((ND, sum_rows(g), 256), F32) for g in range(3)] * 2
        + [V((NL, 2 * w, 256), F32) for w in widths] * 2
        + [V((NL, w, 256), F32) for w in widths]
        + [V((ND, w, NL, 256), F32) for w in widths]
        + [V((ND, b, 16, CW), BF) for b in blocks] * 2
        + [V((NL, 16, CW), BF) for _ in blocks] * 2
        + [V((CW, CW), BF) for _ in blocks]
        + [V((n, CW, CW), BF) for n in (NL, 6)]
        + [dma((3,)), dma((8,)), dma((3,)), dma, dma, dma, dma, dma((NC,)), dma((5, 4)), dma((5, 4))]
    )
    return pl.pallas_call(
        refine_kernel,
        out_shape=out_shape,
        in_specs=[pl.BlockSpec(memory_space=pltpu.VMEM), pl.BlockSpec(memory_space=pltpu.SMEM)] + [anyspace] * 4,
        out_specs=[anyspace] * 4,
        scratch_shapes=scratch,
        compiler_params=pltpu.CompilerParams(
            collective_id=0, has_side_effects=True, vmem_limit_bytes=60 << 20),
    )(ids, fill, vectors, codes, centroids, codebooks)


def finish_kernel(
    err_in, books_in, ga_in, gb_in, err_out, books_out, gram_out, err, books, ga, gb, gram, in_sem, out_sem, gram_sem,
):
    parts = in_sem.shape[0] - 1
    rows = err_in.shape[0] // parts

    def pair(src, held, dst, i):
        return pltpu.make_async_copy(src, held, in_sem.at[i]), pltpu.make_async_copy(held, dst, out_sem.at[i])

    moves = []
    for i in range(parts):
        at = pl.ds(i * rows, rows)
        moves.append(pair(err_in.at[at], err.at[at], err_out.at[at], i))
    moves.append(pair(books_in, books, books_out, parts))
    loads = [pltpu.make_async_copy(ga_in, ga, gram_sem.at[0]), pltpu.make_async_copy(gb_in, gb, gram_sem.at[1])]
    for c in loads:
        c.start()
    for first, _ in moves:
        first.start()
    for c in loads:
        c.wait()
    for j in range(NC):
        for i in range(j + 1):
            block = (ga[block_of(j, i)] if j < NC - 1 else gb[i]).astype(F32)
            jr, ir = slice(j * CW, (j + 1) * CW), slice(i * CW, (i + 1) * CW)
            gram[jr, ir] = block
            if i < j:
                gram[ir, jr] = block.T
    out = pltpu.make_async_copy(gram, gram_out, gram_sem.at[0])
    out.start()
    for first, second in moves:
        first.wait()
        second.start()
    for _, second in moves:
        second.wait()
    out.wait()


def finish(err, books, ga, gb):
    anyspace = pl.BlockSpec(memory_space=pl.ANY)
    dma = pltpu.SemaphoreType.DMA
    return pl.pallas_call(
        finish_kernel,
        out_shape=[
            jax.ShapeDtypeStruct(err.shape, BF),
            jax.ShapeDtypeStruct(books.shape, F32),
            jax.ShapeDtypeStruct((768, 768), F32),
        ],
        in_specs=[anyspace] * 4,
        out_specs=[anyspace] * 3,
        scratch_shapes=[
            pltpu.VMEM(err.shape, BF), pltpu.VMEM(books.shape, F32),
            pltpu.VMEM(ga.shape, BF), pltpu.VMEM(gb.shape, BF), pltpu.VMEM((768, 768), F32),
            dma((9,)), dma((9,)), dma((2,)),
        ],
        compiler_params=pltpu.CompilerParams(vmem_limit_bytes=60 << 20),
    )(err, books, ga, gb)


def local(vectors, list_ids, codes, fill_counts, centroids, codebooks):
    codes_t = codes.T.reshape(NC, MC, SLOTS)
    err, books, ga, gb = refine(
        list_ids.reshape(NL, 1, CAP), fill_counts, vectors, codes_t, centroids, codebooks)
    err, books, gram = finish(err, books, ga, gb)
    return err, books.reshape(96, 8, 256), gram


def solution(mesh):
    in_specs = (
        P(("dp", "list"), None),
        P(("dp", "list")),
        P(("dp", "list"), None),
        P(("dp", "list"), None),
        P("list", None),
        P(),
    )
    out_specs = (P(("dp", "list"), None), P(), P())
    return jax.shard_map(local, mesh=mesh, in_specs=in_specs, out_specs=out_specs, check_vma=False)
```

```python
import functools

import jax
import jax.numpy as jnp
from jax import lax
from jax.experimental import pallas as pl
from jax.experimental.pallas import tpu as pltpu
from jax.sharding import PartitionSpec as P

MESH = pl.DeviceIdType.MESH
F32 = jnp.float32
BF = jnp.bfloat16
NL, ND = 16, 8
CAP = 128
SLOTS = NL * CAP
NC = 6
CW = 128
MC = 16
GROUPS = ((0, 1), (2, 3), (4, 5))
GSTEP = 1024
AHEAD = 2


def sum_rows(g):
    return len(GROUPS[g]) * 24


def block_of(j, i):
    return j * (j + 1) // 2 + i


def drain(ref, sem):
    pltpu.make_async_copy(ref, ref, sem).wait()


def refine_kernel(
    ids_ref, fill_ref, vec_hbm, codes_hbm, cent_hbm, books_hbm,
    err_hbm, nb_hbm, ga_hbm, gb_hbm,
    ids_in, ids_s, table, cbuf, gbuf, sbuf, rbuf, vec, codes, books, res, rest, live, acc, err,
    ds0, ds1, ds2, dr0, dr1, dr2, ls0, ls1, ls2, lr0, lr1, lr2,
    as0, as1, as2, ad0, ad1, ad2,
    gsa, gsb, gra, grb, gla, glb, gma, gmb, gta, gtb, gda, gdb,
    load_sem, cent_sem, out_sem, ids_ssem, ids_rsem, self_sem, x_ssem, x_rsem,
    ar_ssem, ar_rsem,
):
    dp = lax.axis_index("dp")
    me = lax.axis_index("list")
    my_y, my_z = me // 4, me % 4

    def list_peer(s):
        t = lax.rem(s * 7, NL)
        return lax.rem(my_y + t // 4, 4) * 4 + lax.rem(my_z + t % 4, 4)

    def dp_peer(s):
        return lax.rem(dp + lax.rem(s + 2, ND - 1) + 1, ND)

    n_cent = cent_sem.shape[0]
    cent_rows = cbuf.shape[0] // n_cent

    def cent_copy(b):
        rows = pl.ds(pl.multiple_of(b * cent_rows, cent_rows), cent_rows)
        return pltpu.make_async_copy(cent_hbm.at[rows], cbuf.at[rows], cent_sem.at[b])

    codes_load = pltpu.make_async_copy(codes_hbm, codes, load_sem.at[0])
    books_load = pltpu.make_async_copy(books_hbm, books, load_sem.at[1])
    vec_load = pltpu.make_async_copy(vec_hbm, vec, load_sem.at[2])
    for b in range(n_cent):
        cent_copy(b).start()
    vec_load.start()
    codes_load.start()
    books_load.start()

    barrier = pltpu.get_barrier_semaphore()

    def greet_list(s, c):
        pl.semaphore_signal(barrier, inc=1, device_id={"list": list_peer(s)}, device_id_type=MESH)
        return c

    def greet_dp(s, c):
        pl.semaphore_signal(barrier, inc=1, device_id={"dp": dp_peer(s)}, device_id_type=MESH)
        return c

    lax.fori_loop(1, NL, greet_list, 0)
    lax.fori_loop(1, ND, greet_dp, 0)

    def send_ids(s, c):
        p = list_peer(s)
        pltpu.make_async_remote_copy(
            src_ref=ids_ref.at[p], dst_ref=ids_in.at[me], send_sem=ids_ssem, recv_sem=ids_rsem,
            device_id={"list": p}, device_id_type=MESH).start()
        return c


    table_rows = table.reshape(4096 * 8, 128)
    gathered_rows = gbuf.reshape(32 * 8, 128)

    def build(b, c):
        cent_copy(b).wait()

        def rows16(r, c):
            row = pl.multiple_of(b * cent_rows + r * 16, 16)
            for j in range(NC):
                v = cbuf[pl.ds(row, 16), j * CW:(j + 1) * CW].astype(F32)
                table_rows[pl.ds(row * 8 + j, 8, stride=8), :] = v[:8]
                table_rows[pl.ds(row * 8 + 64 + j, 8, stride=8), :] = v[8:]
            return c

        return lax.fori_loop(0, cent_rows // 16, rows16, c, unroll=4)

    lax.fori_loop(0, n_cent, build, 0)
    pl.semaphore_wait(barrier, NL + ND - 2)
    lax.fori_loop(1, NL, send_ids, 0)
    ids_in[me] = ids_ref[me]

    lane = lax.broadcasted_iota(jnp.int32, (16, CAP), 1)
    for p in range(NL):
        live[:, p * CAP:(p + 1) * CAP] = (lane < fill_ref[0, p]).astype(F32).astype(BF)

    drain(ids_in.at[pl.ds(0, NL - 1)], ids_rsem)
    drain(ids_in.at[pl.ds(0, NL - 1)], ids_ssem)
    to_smem = pltpu.make_async_copy(ids_in, ids_s, self_sem)
    to_smem.start()
    to_smem.wait()

    def x_copy(j, p):
        return pltpu.make_async_remote_copy(
            src_ref=sbuf.at[j, p], dst_ref=rbuf.at[j, me], send_sem=x_ssem, recv_sem=x_rsem.at[j],
            device_id={"list": p}, device_id_type=MESH)

    def gather(p, dst):
        def rows(r, c):
            for half in range(2):
                for k in range(16):
                    row = ids_s[p, 0, r * 32 + half * 16 + k]
                    gbuf[half * 16 + k] = table[row]
            for half in range(2):
                at = pl.ds(pl.multiple_of(r * 32 + half * 16, 16), 16)
                for j in range(NC):
                    lo = gathered_rows[pl.ds(half * 128 + j, 8, stride=8), :]
                    hi = gathered_rows[pl.ds(half * 128 + 64 + j, 8, stride=8), :]
                    dst[j, p, at, :] = jnp.concatenate([lo, hi], 0).astype(BF)
            return c

        lax.fori_loop(0, CAP // 32, rows, 0)

    def gather_send(s, c):
        p = list_peer(s)
        gather(p, sbuf)
        x_copy(0, p).start()
        return c

    lax.fori_loop(1, NL, gather_send, 0)

    def send_chunk(j):
        def one(s, c):
            x_copy(j, list_peer(s)).start()
            return c

        lax.fori_loop(1, NL, one, 0)

    send_chunk(1)
    gather(me, rbuf)

    vec_load.wait()
    codes_load.wait()
    books_load.wait()

    send_sums = (ds0, ds1, ds2)
    lane128 = lax.broadcasted_iota(jnp.int32, (8, 128), 1)
    row8 = lax.broadcasted_iota(jnp.int32, (8, 128), 0)
    sub16 = lax.broadcasted_iota(jnp.int32, (16, GSTEP), 0)
    sub16_f = sub16.astype(F32).astype(BF)
    sub16_h = (sub16 // 4).astype(F32).astype(BF)

    def residual_chunk(j):
        def one(p, c):
            rows = pl.ds(pl.multiple_of(p * CAP, CAP), CAP)
            v = vec[rows, pl.ds(pl.multiple_of(j * CW, CW), CW)].astype(F32)
            d = v - rbuf[j, p].astype(F32)
            keep = lax.broadcasted_iota(jnp.int32, (CAP, CW), 0) < fill_ref[0, p]
            d = jnp.where(keep, d, 0.0).astype(BF)
            res[j, rows, :] = d
            rest[j, :, pl.ds(pl.multiple_of(p * CAP, CAP), CAP)] = d.T
            return c

        lax.fori_loop(0, NL, one, 0, unroll=4)

    def hist_chunk(g, u, j):
        acc[...] = jnp.zeros_like(acc)

        def step(t, c):
            gs = pl.ds(pl.multiple_of(t * GSTEP, GSTEP), GSTEP)
            code = codes[j, :, gs]
            hi_all = (code >> 6).astype(F32)
            lo_all = (code & 63).astype(F32)
            alive = live[:, gs]
            zero = jnp.zeros((16, GSTEP), BF)
            one = jnp.ones((16, GSTEP), BF)
            for grp in range(4):
                left = []
                for pair in range(2):
                    m = grp * 4 + pair * 2
                    hi2 = jnp.concatenate([
                        jnp.broadcast_to(hi_all[m:m + 1], (8, GSTEP)),
                        jnp.broadcast_to(hi_all[m + 1:m + 2], (8, GSTEP))], 0).astype(BF)
                    r16 = rest[j, m * 8:m * 8 + 16, gs]
                    for h in range(4):
                        left.append(jnp.where(hi2 == jnp.array(h, BF), r16, zero))
                hi4 = hi_all[grp * 4:grp * 4 + 4]
                hi4 = jnp.concatenate([hi4, hi4, hi4, hi4], 0).astype(BF)
                left.append(jnp.where(hi4 == sub16_h, alive, zero))
                right = []
                for ml in range(4):
                    m = grp * 4 + ml
                    lo = jnp.broadcast_to(lo_all[m:m + 1], (16, GSTEP)).astype(BF)
                    for t16 in range(4):
                        right.append(jnp.where(lo == sub16_f + jnp.array(16 * t16, BF), one, zero))
                acc[grp] += lax.dot_general(
                    jnp.concatenate(left, 0), jnp.concatenate(right, 0),
                    (((1,), (1,)), ((), ())), preferred_element_type=F32)
            return c

        lax.fori_loop(0, SLOTS // GSTEP, step, 0)
        buf = send_sums[g]
        base = pl.multiple_of(u * 24, 8)
        for grp in range(4):
            for pair in range(2):
                q = grp * 2 + pair
                tile = slice(pair * 128, pair * 128 + 128)
                for t in range(2):
                    out = slice(t * 128, t * 128 + 128)
                    cnt = []
                    for m2 in range(2):
                        halves = []
                        for h, here in ((2 * t, m2 == 0), (2 * t + 1, m2 == 1)):
                            at = pair * 64 + h * 16 + m2 * 8
                            row = 128 + h * 4 + pair * 2 + m2
                            s = acc[grp, at:at + 8, tile]
                            n = jnp.broadcast_to(acc[grp, row:row + 1, tile], (8, 128))
                            if not here:
                                s = pltpu.roll(s, 64, 1)
                                n = pltpu.roll(n, 64, 1)
                            halves.append((s, n))
                        buf[q, pl.ds(base + m2 * 8, 8), out] = jnp.where(lane128 < 64, halves[0][0], halves[1][0])
                        cnt.append(jnp.where(lane128 < 64, halves[0][1], halves[1][1]))
                    buf[q, pl.ds(base + 16, 8), out] = jnp.where(row8 == 0, cnt[0], cnt[1])

    def gram_chunk(buf, j, first):
        for i in range(0, j + 1, 2):
            wide = min(2, j + 1 - i)
            right = jnp.concatenate([res[i + k] for k in range(wide)], 1)
            block = lax.dot_general(
                rest[j], right, (((1,), (0,)), ((), ())), preferred_element_type=F32) * (1.0 / (SLOTS * NL * ND))
            for k in range(wide):
                for q in range(ND):
                    buf[q, first + i + k] = block[q * 16:q * 16 + 16, k * CW:(k + 1) * CW].astype(BF)

    def start_dp(a, src, dst, part):
        def one(s, c):
            q = dp_peer(s)
            pltpu.make_async_remote_copy(
                src_ref=src.at[q, part], dst_ref=dst.at[dp, part], send_sem=ar_ssem.at[a, 0],
                recv_sem=ar_rsem.at[a, 0], device_id={"dp": q}, device_id_type=MESH).start()
            return c

        lax.fori_loop(1, ND, one, 0)

    def start_list(a, src, dst):
        def one(s, c):
            p = list_peer(s)
            pltpu.make_async_remote_copy(
                src_ref=src.at[p], dst_ref=dst.at[me], send_sem=ar_ssem.at[a, 1], recv_sem=ar_rsem.at[a, 1],
                device_id={"list": p}, device_id_type=MESH).start()
            return c

        lax.fori_loop(1, NL, one, 0)

    def share_list(a, buf):
        def one(s, c):
            pltpu.make_async_remote_copy(
                src_ref=buf.at[me], dst_ref=buf.at[me], send_sem=ar_ssem.at[a, 2], recv_sem=ar_rsem.at[a, 2],
                device_id={"list": list_peer(s)}, device_id_type=MESH).start()
            return c

        lax.fori_loop(1, NL, one, 0)

    def share_dp(a, buf):
        def one(s, c):
            pltpu.make_async_remote_copy(
                src_ref=buf.at[dp], dst_ref=buf.at[dp], send_sem=ar_ssem.at[a, 3], recv_sem=ar_rsem.at[a, 3],
                device_id={"dp": dp_peer(s)}, device_id_type=MESH).start()
            return c

        lax.fori_loop(1, ND, one, 0)

    recv_sums, ls, lr, ag, ad = (dr0, dr1, dr2), (ls0, ls1, ls2), (lr0, lr1, lr2), (as0, as1, as2), (ad0, ad1, ad2)

    def sums_1(g, u):
        start_dp(g, send_sums[g], recv_sums[g], pl.ds(u * 24, 24))

    def sums_2(g):
        src, dst, width = send_sums[g], recv_sums[g], len(GROUPS[g])
        drain(dst.at[pl.ds(0, ND - 1)], ar_rsem.at[g, 0])
        dst[dp] = src[dp]
        total = dst[0]
        for q in range(1, ND):
            total = total + dst[q]
        for u in range(width):
            for p in range(NL):
                ls[g][p, u:u + 1, :] = total[u * 24 + p:u * 24 + p + 1]
                at = u * 24 + 16 + p // 8
                ls[g][p, width + u:width + u + 1, :] = total[at:at + 1]
        start_list(g, ls[g], lr[g])

    def sums_3(g):
        width = len(GROUPS[g])
        drain(lr[g].at[pl.ds(0, NL - 1)], ar_rsem.at[g, 1])
        lr[g][me] = ls[g][me]
        total = lr[g][0]
        for p in range(1, NL):
            total = total + lr[g][p]
        for u in range(width):
            m = GROUPS[g][u] * MC + dp * 2 + me // 8
            old = books[m, pl.ds(lax.rem(me, 8), 1), :]
            ag[g][me, u:u + 1, :] = (total[u:u + 1] + old) / (total[width + u:width + u + 1] + 1.0)
        share_list(g, ag[g])

    def sums_4(g):
        drain(ag[g].at[pl.ds(0, NL - 1)], ar_rsem.at[g, 2])
        for u in range(len(GROUPS[g])):
            for p in range(NL):
                ad[g][dp, u, p:p + 1, :] = ag[g][p, u:u + 1, :]
        share_dp(g, ad[g])

    def sums_5(g):
        drain(ad[g].at[pl.ds(0, ND - 1)], ar_rsem.at[g, 3])

    gs_, gr_, gl_, gm_, gt_, gd_ = (gsa, gsb), (gra, grb), (gla, glb), (gma, gmb), (gta, gtb), (gda, gdb)

    def gram_1(k, first, count):
        start_dp(3 + k, gs_[k], gr_[k], pl.ds(first, count))

    def gram_2(k):
        drain(gr_[k].at[pl.ds(0, ND - 1)], ar_rsem.at[3 + k, 0])
        blocks = gs_[k].shape[1]

        def one(b, c):
            total = gs_[k][dp, b].astype(F32)
            for s in range(1, ND):
                total = total + gr_[k][dp_peer(s), b].astype(F32)
            gl_[k][b] = total.astype(BF)
            return c

        lax.fori_loop(0, blocks, one, 0)
        for b in range(blocks, NL):
            gl_[k][b] = jnp.zeros((16, CW), BF)
        start_list(3 + k, gl_[k], gm_[k])

    def gram_3(k):
        drain(gm_[k].at[pl.ds(0, NL - 1)], ar_rsem.at[3 + k, 1])
        total = gl_[k][me].astype(F32)
        for s in range(1, NL):
            total = total + gm_[k][list_peer(s)].astype(F32)
        mine = pl.ds(pl.multiple_of(dp * 16, 16), 16)
        gt_[k][mine, :] = total.astype(BF)

        def one(s, c):
            pltpu.make_async_remote_copy(
                src_ref=gt_[k].at[mine], dst_ref=gt_[k].at[mine], send_sem=ar_ssem.at[3 + k, 2],
                recv_sem=ar_rsem.at[3 + k, 2], device_id={"dp": dp_peer(s)}, device_id_type=MESH).start()
            return c

        lax.fori_loop(1, ND, one, 0)

    def with_block(k, yes, no=None):
        owners = gd_[k].shape[0]
        if owners == NL:
            yes()
        else:
            pl.when(me < owners)(yes)
            if no is not None:
                pl.when(me >= owners)(no)

    def gram_4(k):
        drain(gt_[k].at[pl.ds(0, 112)], ar_rsem.at[3 + k, 2])

        def send():
            gd_[k][me] = gt_[k][...]

            def one(s, c):
                pltpu.make_async_remote_copy(
                    src_ref=gt_[k], dst_ref=gd_[k].at[me], send_sem=ar_ssem.at[3 + k, 3],
                    recv_sem=ar_rsem.at[3 + k, 3], device_id={"list": list_peer(s)}, device_id_type=MESH).start()
                return c

            lax.fori_loop(1, NL, one, 0)

        with_block(k, send)

    def gram_5(k):
        owners = gd_[k].shape[0]
        with_block(
            k,
            lambda: drain(gd_[k].at[pl.ds(0, owners - 1)], ar_rsem.at[3 + k, 3]),
            lambda: drain(gd_[k], ar_rsem.at[3 + k, 3]))

    def err_out(j):
        return pltpu.make_async_copy(
            err.at[j], err_hbm.at[:, pl.ds(pl.multiple_of(j * CW, CW), CW)], out_sem.at[0])

    def error_chunk(g, u, j):
        def one(p, c):
            at = pl.ds(pl.multiple_of(p * CAP, CAP), CAP)
            used = lane128 < fill_ref[0, p]
            parts = []
            for m in range(MC):
                code = jnp.broadcast_to(codes[j, m:m + 1, at], (8, 128))
                k = code & 127
                t = ad[g][m // 2, u, (m % 2) * 8:(m % 2) * 8 + 8, :]
                lo = jnp.take_along_axis(t[:, :128], k, axis=1, mode="promise_in_bounds")
                hi = jnp.take_along_axis(t[:, 128:], k, axis=1, mode="promise_in_bounds")
                r = rest[j, m * 8:m * 8 + 8, at].astype(F32)
                parts.append(jnp.where(used, r - jnp.where(code < 128, lo, hi), 0.0))
            err[j, at, :] = jnp.concatenate(parts, 0).astype(BF).T
            return c

        lax.fori_loop(0, NL, one, 0, unroll=4)
        err_out(j).start()

    def book_outs(g):
        return [pltpu.make_async_copy(ad[g].at[:, u], nb_hbm.at[j], out_sem.at[1]) for u, j in enumerate(GROUPS[g])]

    def chunk(g, u, j, arrived=None):
        drain(rbuf.at[j, pl.ds(0, NL - 1)], x_rsem.at[j])
        if arrived is not None:
            arrived(0)
        if j + AHEAD < NC:
            send_chunk(j + AHEAD)
        residual_chunk(j)
        hist_chunk(g, u, j)

    def gram_early(j):
        gram_chunk(gsa, j, block_of(j, 0))
        gram_1(0, block_of(j, 0), j + 1)

    chunk(0, 0, 0)
    sums_1(0, 0)
    gram_early(0)
    chunk(0, 1, 1)
    sums_1(0, 1)
    gram_early(1)
    chunk(1, 0, 2)
    sums_1(1, 0)
    gram_early(2)
    chunk(1, 1, 3, sums_2)
    sums_1(1, 1)
    gram_early(3)
    chunk(2, 0, 4, sums_3)
    sums_1(2, 0)
    gram_early(4)
    chunk(2, 1, 5, lambda g: (sums_4(0), sums_2(1)))
    sums_1(2, 1)
    gram_chunk(gsb, NC - 1, 0)
    gram_1(1, 0, NC)
    gram_2(0)
    sums_3(1)
    sums_2(2)
    gram_2(1)
    sums_5(0)
    error_chunk(0, 0, 0)
    sums_4(1)
    sums_3(2)
    gram_3(0)
    gram_3(1)
    error_chunk(0, 1, 1)
    sums_4(2)
    gram_4(1)
    gram_4(0)
    sums_5(1)
    error_chunk(1, 0, 2)
    error_chunk(1, 1, 3)
    sums_5(2)
    error_chunk(2, 0, 4)
    error_chunk(2, 1, 5)
    gram_5(1)
    gram_5(0)
    outs = [o for g in range(3) for o in book_outs(g)]
    outs += [pltpu.make_async_copy(gda, ga_hbm, out_sem.at[2]), pltpu.make_async_copy(gdb, gb_hbm, out_sem.at[2])]
    for o in outs:
        o.start()
    for j in range(NC):
        drain(sbuf.at[j, pl.ds(0, NL - 1)], x_ssem)
    for g in range(3):
        drain(send_sums[g].at[pl.ds(0, ND - 1)], ar_ssem.at[g, 0])
        drain(ls[g].at[pl.ds(0, NL - 1)], ar_ssem.at[g, 1])
        drain(ag[g].at[pl.ds(0, NL - 1)], ar_ssem.at[g, 2])
        drain(ad[g].at[pl.ds(0, ND - 1)], ar_ssem.at[g, 3])
    for k in range(2):
        drain(gs_[k].at[pl.ds(0, ND - 1)], ar_ssem.at[3 + k, 0])
        drain(gl_[k].at[pl.ds(0, NL - 1)], ar_ssem.at[3 + k, 1])
        drain(gt_[k].at[pl.ds(0, 112)], ar_ssem.at[3 + k, 2])
        with_block(k, lambda: drain(gda.at[pl.ds(0, NL - 1)], ar_ssem.at[3 + k, 3]))
    for j in range(NC):
        err_out(j).wait()
    for o in outs:
        o.wait()


def refine(ids, fill, vectors, codes, centroids, codebooks):
    anyspace = pl.BlockSpec(memory_space=pl.ANY)
    V = pltpu.VMEM
    widths = [len(g) for g in GROUPS]
    blocks = (15, 6)
    dma = pltpu.SemaphoreType.DMA
    out_shape = [
        jax.ShapeDtypeStruct((SLOTS, 768), BF),
        jax.ShapeDtypeStruct((NC, ND, 16, 256), F32),
        jax.ShapeDtypeStruct((NL, CW, CW), BF),
        jax.ShapeDtypeStruct((6, CW, CW), BF),
    ]
    scratch = (
        [
            V((NL, 1, CAP), jnp.int32), pltpu.SMEM((NL, 1, CAP), jnp.int32),
            V((4096, 8, 128), F32), V((4096, 768), BF), V((32, 8, 128), F32),
            V((NC, NL, CAP, CW), BF), V((NC, NL, CAP, CW), BF),
            V((SLOTS, 768), BF), V((NC, MC, SLOTS), jnp.int32), V((96, 8, 256), F32),
            V((NC, SLOTS, CW), BF), V((NC, CW, SLOTS), BF), V((16, SLOTS), BF), V((4, 144, 256), F32),
            V((NC, SLOTS, CW), BF),
        ]
        + [V((ND, sum_rows(g), 256), F32) for g in range(3)] * 2
        + [V((NL, 2 * w, 256), F32) for w in widths] * 2
        + [V((NL, w, 256), F32) for w in widths]
        + [V((ND, w, NL, 256), F32) for w in widths]
        + [V((ND, b, 16, CW), BF) for b in blocks] * 2
        + [V((NL, 16, CW), BF) for _ in blocks] * 2
        + [V((CW, CW), BF) for _ in blocks]
        + [V((n, CW, CW), BF) for n in (NL, 6)]
        + [dma((3,)), dma((8,)), dma((3,)), dma, dma, dma, dma, dma((NC,)), dma((5, 4)), dma((5, 4))]
    )
    return pl.pallas_call(
        refine_kernel,
        out_shape=out_shape,
        in_specs=[pl.BlockSpec(memory_space=pltpu.VMEM), pl.BlockSpec(memory_space=pltpu.SMEM)] + [anyspace] * 4,
        out_specs=[anyspace] * 4,
        scratch_shapes=scratch,
        compiler_params=pltpu.CompilerParams(
            collective_id=0, has_side_effects=True, vmem_limit_bytes=60 << 20),
    )(ids, fill, vectors, codes, centroids, codebooks)


def finish_kernel(
    err_in, books_in, ga_in, gb_in, err_out, books_out, gram_out, err, books, ga, gb, gram, in_sem, out_sem, gram_sem,
):
    parts = in_sem.shape[0] - 1
    rows = err_in.shape[0] // parts

    def pair(src, held, dst, i):
        return pltpu.make_async_copy(src, held, in_sem.at[i]), pltpu.make_async_copy(held, dst, out_sem.at[i])

    moves = []
    for i in range(parts):
        at = pl.ds(i * rows, rows)
        moves.append(pair(err_in.at[at], err.at[at], err_out.at[at], i))
    moves.append(pair(books_in, books, books_out, parts))
    loads = [pltpu.make_async_copy(ga_in, ga, gram_sem.at[0]), pltpu.make_async_copy(gb_in, gb, gram_sem.at[1])]
    for c in loads:
        c.start()
    for first, _ in moves:
        first.start()
    for c in loads:
        c.wait()
    for j in range(NC):
        for i in range(j + 1):
            block = (ga[block_of(j, i)] if j < NC - 1 else gb[i]).astype(F32)
            jr, ir = slice(j * CW, (j + 1) * CW), slice(i * CW, (i + 1) * CW)
            gram[jr, ir] = block
            if i < j:
                gram[ir, jr] = block.T
    out = pltpu.make_async_copy(gram, gram_out, gram_sem.at[0])
    out.start()
    for first, second in moves:
        first.wait()
        second.start()
    for _, second in moves:
        second.wait()
    out.wait()


def finish(err, books, ga, gb):
    anyspace = pl.BlockSpec(memory_space=pl.ANY)
    dma = pltpu.SemaphoreType.DMA
    return pl.pallas_call(
        finish_kernel,
        out_shape=[
            jax.ShapeDtypeStruct(err.shape, BF),
            jax.ShapeDtypeStruct(books.shape, F32),
            jax.ShapeDtypeStruct((768, 768), F32),
        ],
        in_specs=[anyspace] * 4,
        out_specs=[anyspace] * 3,
        scratch_shapes=[
            pltpu.VMEM(err.shape, BF), pltpu.VMEM(books.shape, F32),
            pltpu.VMEM(ga.shape, BF), pltpu.VMEM(gb.shape, BF), pltpu.VMEM((768, 768), F32),
            dma((9,)), dma((9,)), dma((2,)),
        ],
        compiler_params=pltpu.CompilerParams(vmem_limit_bytes=60 << 20),
    )(err, books, ga, gb)


def local(vectors, list_ids, codes, fill_counts, centroids, codebooks):
    codes_t = codes.T.reshape(NC, MC, SLOTS)
    err, books, ga, gb = refine(
        list_ids.reshape(NL, 1, CAP), fill_counts, vectors, codes_t, centroids, codebooks)
    err, books, gram = finish(err, books, ga, gb)
    return err, books.reshape(96, 8, 256), gram


def solution(mesh):
    in_specs = (
        P(("dp", "list"), None),
        P(("dp", "list")),
        P(("dp", "list"), None),
        P(("dp", "list"), None),
        P("list", None),
        P(),
    )
    out_specs = (P(("dp", "list"), None), P(), P())
    return jax.shard_map(local, mesh=mesh, in_specs=in_specs, out_specs=out_specs, check_vma=False)
```

```python
import functools

import jax
import jax.numpy as jnp
from jax import lax
from jax.experimental import pallas as pl
from jax.experimental.pallas import tpu as pltpu
from jax.sharding import PartitionSpec as P

MESH = pl.DeviceIdType.MESH
F32 = jnp.float32
BF = jnp.bfloat16
NL, ND = 16, 8
CAP = 128
SLOTS = NL * CAP
NC = 6
CW = 128
MC = 16
GROUPS = ((0, 1), (2, 3), (4, 5))
GSTEP = 1024
AHEAD = 2


def sum_rows(g):
    return len(GROUPS[g]) * 24


def block_of(j, i):
    return j * (j + 1) // 2 + i


def drain(ref, sem):
    pltpu.make_async_copy(ref, ref, sem).wait()


def refine_kernel(
    ids_ref, fill_ref, vec_hbm, codes_hbm, cent_hbm, books_hbm,
    err_hbm, nb_hbm, ga_hbm, gb_hbm,
    ids_in, ids_s, table, cbuf, gbuf, sbuf, rbuf, vec, codes, books, res, rest, live, acc, err,
    ds0, ds1, ds2, dr0, dr1, dr2, ls0, ls1, ls2, lr0, lr1, lr2,
    as0, as1, as2, ad0, ad1, ad2,
    gsa, gsb, gra, grb, gla, glb, gma, gmb, gta, gtb, gda, gdb,
    load_sem, cent_sem, out_sem, ids_ssem, ids_rsem, self_sem, x_ssem, x_rsem,
    ar_ssem, ar_rsem,
):
    dp = lax.axis_index("dp")
    me = lax.axis_index("list")
    my_y, my_z = me // 4, me % 4

    def list_peer(s):
        t = lax.rem(s * 7, NL)
        return lax.rem(my_y + t // 4, 4) * 4 + lax.rem(my_z + t % 4, 4)

    def dp_peer(s):
        return lax.rem(dp + lax.rem(s + 2, ND - 1) + 1, ND)

    n_cent = cent_sem.shape[0]
    cent_rows = cbuf.shape[0] // n_cent

    def cent_copy(b):
        rows = pl.ds(pl.multiple_of(b * cent_rows, cent_rows), cent_rows)
        return pltpu.make_async_copy(cent_hbm.at[rows], cbuf.at[rows], cent_sem.at[b])

    codes_load = pltpu.make_async_copy(codes_hbm, codes, load_sem.at[0])
    books_load = pltpu.make_async_copy(books_hbm, books, load_sem.at[1])
    vec_load = pltpu.make_async_copy(vec_hbm, vec, load_sem.at[2])
    for b in range(n_cent):
        cent_copy(b).start()
    vec_load.start()
    codes_load.start()
    books_load.start()

    barrier = pltpu.get_barrier_semaphore()

    def greet_list(s, c):
        pl.semaphore_signal(barrier, inc=1, device_id={"list": list_peer(s)}, device_id_type=MESH)
        return c

    def greet_dp(s, c):
        pl.semaphore_signal(barrier, inc=1, device_id={"dp": dp_peer(s)}, device_id_type=MESH)
        return c

    lax.fori_loop(1, NL, greet_list, 0)
    lax.fori_loop(1, ND, greet_dp, 0)

    def send_ids(s, c):
        p = list_peer(s)
        pltpu.make_async_remote_copy(
            src_ref=ids_ref.at[p], dst_ref=ids_in.at[me], send_sem=ids_ssem, recv_sem=ids_rsem,
            device_id={"list": p}, device_id_type=MESH).start()
        return c


    table_rows = table.reshape(4104 * 8, 128)
    gathered_rows = gbuf.reshape(40 * 8, 128)

    def build(b, c):
        cent_copy(b).wait()

        def rows16(r, c):
            row = pl.multiple_of(b * cent_rows + r * 16, 16)
            for j in range(NC):
                v = cbuf[pl.ds(row, 16), j * CW:(j + 1) * CW].astype(F32)
                table_rows[pl.ds(row * 8 + j, 8, stride=8), :] = v[:8]
                table_rows[pl.ds(row * 8 + 64 + j, 8, stride=8), :] = v[8:]
            return c

        return lax.fori_loop(0, cent_rows // 16, rows16, c, unroll=4)

    lax.fori_loop(0, n_cent, build, 0)
    pl.semaphore_wait(barrier, NL + ND - 2)
    lax.fori_loop(1, NL, send_ids, 0)
    ids_in[me] = ids_ref[me]

    lane = lax.broadcasted_iota(jnp.int32, (16, CAP), 1)
    for p in range(NL):
        live[:, p * CAP:(p + 1) * CAP] = (lane < fill_ref[0, p]).astype(F32).astype(BF)

    drain(ids_in.at[pl.ds(0, NL - 1)], ids_rsem)
    drain(ids_in.at[pl.ds(0, NL - 1)], ids_ssem)
    to_smem = pltpu.make_async_copy(ids_in, ids_s, self_sem)
    to_smem.start()
    to_smem.wait()

    def x_copy(j, p):
        return pltpu.make_async_remote_copy(
            src_ref=sbuf.at[j, p], dst_ref=rbuf.at[j, me], send_sem=x_ssem, recv_sem=x_rsem.at[j],
            device_id={"list": p}, device_id_type=MESH)

    def gather(p, dst):
        def rows(r, c):
            for half in range(2):
                for k in range(16):
                    row = ids_s[p, 0, r * 32 + half * 16 + k]
                    gbuf[half * 16 + k] = table[row]
            for half in range(2):
                at = pl.ds(pl.multiple_of(r * 32 + half * 16, 16), 16)
                for j in range(NC):
                    lo = gathered_rows[pl.ds(half * 128 + j, 8, stride=8), :]
                    hi = gathered_rows[pl.ds(half * 128 + 64 + j, 8, stride=8), :]
                    dst[j, p, at, :] = jnp.concatenate([lo, hi], 0).astype(BF)
            return c

        lax.fori_loop(0, CAP // 32, rows, 0)

    def gather_send(s, c):
        p = list_peer(s)
        gather(p, sbuf)
        x_copy(0, p).start()
        return c

    lax.fori_loop(1, NL, gather_send, 0)

    def send_chunk(j):
        def one(s, c):
            x_copy(j, list_peer(s)).start()
            return c

        lax.fori_loop(1, NL, one, 0)

    send_chunk(1)
    gather(me, rbuf)

    vec_load.wait()
    codes_load.wait()
    books_load.wait()

    send_sums = (ds0, ds1, ds2)
    lane128 = lax.broadcasted_iota(jnp.int32, (8, 128), 1)
    row8 = lax.broadcasted_iota(jnp.int32, (8, 128), 0)
    sub16 = lax.broadcasted_iota(jnp.int32, (16, GSTEP), 0)
    sub16_f = sub16.astype(F32).astype(BF)
    sub16_h = (sub16 // 4).astype(F32).astype(BF)

    def residual_chunk(j):
        def one(p, c):
            rows = pl.ds(pl.multiple_of(p * CAP, CAP), CAP)
            v = vec[rows, pl.ds(pl.multiple_of(j * CW, CW), CW)].astype(F32)
            d = v - rbuf[j, p].astype(F32)
            keep = lax.broadcasted_iota(jnp.int32, (CAP, CW), 0) < fill_ref[0, p]
            d = jnp.where(keep, d, 0.0).astype(BF)
            res[j, rows, :] = d
            rest[j, :, pl.ds(pl.multiple_of(p * CAP, CAP), CAP)] = d.T
            return c

        lax.fori_loop(0, NL, one, 0, unroll=4)

    def hist_chunk(g, u, j):
        acc[...] = jnp.zeros_like(acc)

        def step(t, c):
            gs = pl.ds(pl.multiple_of(t * GSTEP, GSTEP), GSTEP)
            code = codes[j, :, gs]
            hi_all = (code >> 6).astype(F32)
            lo_all = (code & 63).astype(F32)
            alive = live[:, gs]
            zero = jnp.zeros((16, GSTEP), BF)
            one = jnp.ones((16, GSTEP), BF)
            for grp in range(4):
                left = []
                for pair in range(2):
                    m = grp * 4 + pair * 2
                    hi2 = jnp.concatenate([
                        jnp.broadcast_to(hi_all[m:m + 1], (8, GSTEP)),
                        jnp.broadcast_to(hi_all[m + 1:m + 2], (8, GSTEP))], 0).astype(BF)
                    r16 = rest[j, m * 8:m * 8 + 16, gs]
                    for h in range(4):
                        left.append(jnp.where(hi2 == jnp.array(h, BF), r16, zero))
                hi4 = hi_all[grp * 4:grp * 4 + 4]
                hi4 = jnp.concatenate([hi4, hi4, hi4, hi4], 0).astype(BF)
                left.append(jnp.where(hi4 == sub16_h, alive, zero))
                right = []
                for ml in range(4):
                    m = grp * 4 + ml
                    lo = jnp.broadcast_to(lo_all[m:m + 1], (16, GSTEP)).astype(BF)
                    for t16 in range(4):
                        right.append(jnp.where(lo == sub16_f + jnp.array(16 * t16, BF), one, zero))
                acc[grp] += lax.dot_general(
                    jnp.concatenate(left, 0), jnp.concatenate(right, 0),
                    (((1,), (1,)), ((), ())), preferred_element_type=F32)
            return c

        lax.fori_loop(0, SLOTS // GSTEP, step, 0)
        buf = send_sums[g]
        base = pl.multiple_of(u * 24, 8)
        for grp in range(4):
            for pair in range(2):
                q = grp * 2 + pair
                tile = slice(pair * 128, pair * 128 + 128)
                for t in range(2):
                    out = slice(t * 128, t * 128 + 128)
                    cnt = []
                    for m2 in range(2):
                        halves = []
                        for h, here in ((2 * t, m2 == 0), (2 * t + 1, m2 == 1)):
                            at = pair * 64 + h * 16 + m2 * 8
                            row = 128 + h * 4 + pair * 2 + m2
                            s = acc[grp, at:at + 8, tile]
                            n = jnp.broadcast_to(acc[grp, row:row + 1, tile], (8, 128))
                            if not here:
                                s = pltpu.roll(s, 64, 1)
                                n = pltpu.roll(n, 64, 1)
                            halves.append((s, n))
                        buf[q, pl.ds(base + m2 * 8, 8), out] = jnp.where(lane128 < 64, halves[0][0], halves[1][0])
                        cnt.append(jnp.where(lane128 < 64, halves[0][1], halves[1][1]))
                    buf[q, pl.ds(base + 16, 8), out] = jnp.where(row8 == 0, cnt[0], cnt[1])

    def gram_chunk(buf, j, first):
        for i in range(0, j + 1, 2):
            wide = min(2, j + 1 - i)
            right = jnp.concatenate([res[i + k] for k in range(wide)], 1)
            block = lax.dot_general(
                rest[j], right, (((1,), (0,)), ((), ())), preferred_element_type=F32) * (1.0 / (SLOTS * NL * ND))
            for k in range(wide):
                for q in range(ND):
                    buf[q, first + i + k] = block[q * 16:q * 16 + 16, k * CW:(k + 1) * CW].astype(BF)

    def start_dp(a, src, dst, part):
        def one(s, c):
            q = dp_peer(s)
            pltpu.make_async_remote_copy(
                src_ref=src.at[q, part], dst_ref=dst.at[dp, part], send_sem=ar_ssem.at[a, 0],
                recv_sem=ar_rsem.at[a, 0], device_id={"dp": q}, device_id_type=MESH).start()
            return c

        lax.fori_loop(1, ND, one, 0)

    def start_list(a, src, dst):
        def one(s, c):
            p = list_peer(s)
            pltpu.make_async_remote_copy(
                src_ref=src.at[p], dst_ref=dst.at[me], send_sem=ar_ssem.at[a, 1], recv_sem=ar_rsem.at[a, 1],
                device_id={"list": p}, device_id_type=MESH).start()
            return c

        lax.fori_loop(1, NL, one, 0)

    def share_list(a, buf):
        def one(s, c):
            pltpu.make_async_remote_copy(
                src_ref=buf.at[me], dst_ref=buf.at[me], send_sem=ar_ssem.at[a, 2], recv_sem=ar_rsem.at[a, 2],
                device_id={"list": list_peer(s)}, device_id_type=MESH).start()
            return c

        lax.fori_loop(1, NL, one, 0)

    def share_dp(a, buf):
        def one(s, c):
            pltpu.make_async_remote_copy(
                src_ref=buf.at[dp], dst_ref=buf.at[dp], send_sem=ar_ssem.at[a, 3], recv_sem=ar_rsem.at[a, 3],
                device_id={"dp": dp_peer(s)}, device_id_type=MESH).start()
            return c

        lax.fori_loop(1, ND, one, 0)

    recv_sums, ls, lr, ag, ad = (dr0, dr1, dr2), (ls0, ls1, ls2), (lr0, lr1, lr2), (as0, as1, as2), (ad0, ad1, ad2)

    def sums_1(g, u):
        start_dp(g, send_sums[g], recv_sums[g], pl.ds(u * 24, 24))

    def sums_2(g):
        src, dst, width = send_sums[g], recv_sums[g], len(GROUPS[g])
        drain(dst.at[pl.ds(0, ND - 1)], ar_rsem.at[g, 0])
        dst[dp] = src[dp]
        total = dst[0]
        for q in range(1, ND):
            total = total + dst[q]
        for u in range(width):
            for p in range(NL):
                ls[g][p, u:u + 1, :] = total[u * 24 + p:u * 24 + p + 1]
                at = u * 24 + 16 + p // 8
                ls[g][p, width + u:width + u + 1, :] = total[at:at + 1]
        start_list(g, ls[g], lr[g])

    def sums_3(g):
        width = len(GROUPS[g])
        drain(lr[g].at[pl.ds(0, NL - 1)], ar_rsem.at[g, 1])
        lr[g][me] = ls[g][me]
        total = lr[g][0]
        for p in range(1, NL):
            total = total + lr[g][p]
        for u in range(width):
            m = GROUPS[g][u] * MC + dp * 2 + me // 8
            old = books[m, pl.ds(lax.rem(me, 8), 1), :]
            ag[g][me, u:u + 1, :] = (total[u:u + 1] + old) / (total[width + u:width + u + 1] + 1.0)
        share_list(g, ag[g])

    def sums_4(g):
        drain(ag[g].at[pl.ds(0, NL - 1)], ar_rsem.at[g, 2])
        for u in range(len(GROUPS[g])):
            for p in range(NL):
                ad[g][dp, u, p:p + 1, :] = ag[g][p, u:u + 1, :]
        share_dp(g, ad[g])

    def sums_5(g):
        drain(ad[g].at[pl.ds(0, ND - 1)], ar_rsem.at[g, 3])

    gs_, gr_, gl_, gm_, gt_, gd_ = (gsa, gsb), (gra, grb), (gla, glb), (gma, gmb), (gta, gtb), (gda, gdb)

    def gram_1(k, first, count):
        start_dp(3 + k, gs_[k], gr_[k], pl.ds(first, count))

    def gram_2(k):
        drain(gr_[k].at[pl.ds(0, ND - 1)], ar_rsem.at[3 + k, 0])
        blocks = gs_[k].shape[1]

        def one(b, c):
            total = gs_[k][dp, b].astype(F32)
            for s in range(1, ND):
                total = total + gr_[k][dp_peer(s), b].astype(F32)
            gl_[k][b] = total.astype(BF)
            return c

        lax.fori_loop(0, blocks, one, 0)
        for b in range(blocks, NL):
            gl_[k][b] = jnp.zeros((16, CW), BF)
        start_list(3 + k, gl_[k], gm_[k])

    def gram_3(k):
        drain(gm_[k].at[pl.ds(0, NL - 1)], ar_rsem.at[3 + k, 1])
        total = gl_[k][me].astype(F32)
        for s in range(1, NL):
            total = total + gm_[k][list_peer(s)].astype(F32)
        mine = pl.ds(pl.multiple_of(dp * 16, 16), 16)
        gt_[k][mine, :] = total.astype(BF)

        def one(s, c):
            pltpu.make_async_remote_copy(
                src_ref=gt_[k].at[mine], dst_ref=gt_[k].at[mine], send_sem=ar_ssem.at[3 + k, 2],
                recv_sem=ar_rsem.at[3 + k, 2], device_id={"dp": dp_peer(s)}, device_id_type=MESH).start()
            return c

        lax.fori_loop(1, ND, one, 0)

    def with_block(k, yes, no=None):
        owners = gd_[k].shape[0]
        if owners == NL:
            yes()
        else:
            pl.when(me < owners)(yes)
            if no is not None:
                pl.when(me >= owners)(no)

    def gram_4(k):
        drain(gt_[k].at[pl.ds(0, 112)], ar_rsem.at[3 + k, 2])

        def send():
            gd_[k][me] = gt_[k][...]

            def one(s, c):
                pltpu.make_async_remote_copy(
                    src_ref=gt_[k], dst_ref=gd_[k].at[me], send_sem=ar_ssem.at[3 + k, 3],
                    recv_sem=ar_rsem.at[3 + k, 3], device_id={"list": list_peer(s)}, device_id_type=MESH).start()
                return c

            lax.fori_loop(1, NL, one, 0)

        with_block(k, send)

    def gram_5(k):
        owners = gd_[k].shape[0]
        with_block(
            k,
            lambda: drain(gd_[k].at[pl.ds(0, owners - 1)], ar_rsem.at[3 + k, 3]),
            lambda: drain(gd_[k], ar_rsem.at[3 + k, 3]))

    def err_out(j):
        return pltpu.make_async_copy(
            err.at[j], err_hbm.at[:, pl.ds(pl.multiple_of(j * CW, CW), CW)], out_sem.at[0])

    def error_chunk(g, u, j):
        def one(p, c):
            at = pl.ds(pl.multiple_of(p * CAP, CAP), CAP)
            used = lane128 < fill_ref[0, p]
            parts = []
            for m in range(MC):
                code = jnp.broadcast_to(codes[j, m:m + 1, at], (8, 128))
                k = code & 127
                t = ad[g][m // 2, u, (m % 2) * 8:(m % 2) * 8 + 8, :]
                lo = jnp.take_along_axis(t[:, :128], k, axis=1, mode="promise_in_bounds")
                hi = jnp.take_along_axis(t[:, 128:], k, axis=1, mode="promise_in_bounds")
                r = rest[j, m * 8:m * 8 + 8, at].astype(F32)
                parts.append(jnp.where(used, r - jnp.where(code < 128, lo, hi), 0.0))
            err[j, at, :] = jnp.concatenate(parts, 0).astype(BF).T
            return c

        lax.fori_loop(0, NL, one, 0, unroll=4)
        err_out(j).start()

    def book_outs(g):
        return [pltpu.make_async_copy(ad[g].at[:, u], nb_hbm.at[j], out_sem.at[1]) for u, j in enumerate(GROUPS[g])]

    def chunk(g, u, j, arrived=None):
        drain(rbuf.at[j, pl.ds(0, NL - 1)], x_rsem.at[j])
        if arrived is not None:
            arrived(0)
        if j + AHEAD < NC:
            send_chunk(j + AHEAD)
        residual_chunk(j)
        hist_chunk(g, u, j)

    def gram_early(j):
        gram_chunk(gsa, j, block_of(j, 0))
        gram_1(0, block_of(j, 0), j + 1)

    chunk(0, 0, 0)
    sums_1(0, 0)
    gram_early(0)
    chunk(0, 1, 1)
    sums_1(0, 1)
    gram_early(1)
    chunk(1, 0, 2)
    sums_1(1, 0)
    gram_early(2)
    sums_2(0)
    chunk(1, 1, 3)
    sums_1(1, 1)
    gram_early(3)
    chunk(2, 0, 4, sums_3)
    sums_1(2, 0)
    gram_early(4)
    chunk(2, 1, 5, lambda g: (sums_4(0), sums_2(1)))
    sums_1(2, 1)
    gram_chunk(gsb, NC - 1, 0)
    gram_1(1, 0, NC)
    gram_2(0)
    sums_3(1)
    sums_2(2)
    gram_2(1)
    sums_5(0)
    error_chunk(0, 0, 0)
    sums_4(1)
    sums_3(2)
    gram_3(0)
    gram_3(1)
    error_chunk(0, 1, 1)
    sums_4(2)
    gram_4(1)
    gram_4(0)
    sums_5(1)
    error_chunk(1, 0, 2)
    error_chunk(1, 1, 3)
    sums_5(2)
    error_chunk(2, 0, 4)
    error_chunk(2, 1, 5)
    gram_5(1)
    gram_5(0)
    outs = [o for g in range(3) for o in book_outs(g)]
    outs += [pltpu.make_async_copy(gda, ga_hbm, out_sem.at[2]), pltpu.make_async_copy(gdb, gb_hbm, out_sem.at[2])]
    for o in outs:
        o.start()
    for j in range(NC):
        drain(sbuf.at[j, pl.ds(0, NL - 1)], x_ssem)
    for g in range(3):
        drain(send_sums[g].at[pl.ds(0, ND - 1)], ar_ssem.at[g, 0])
        drain(ls[g].at[pl.ds(0, NL - 1)], ar_ssem.at[g, 1])
        drain(ag[g].at[pl.ds(0, NL - 1)], ar_ssem.at[g, 2])
        drain(ad[g].at[pl.ds(0, ND - 1)], ar_ssem.at[g, 3])
    for k in range(2):
        drain(gs_[k].at[pl.ds(0, ND - 1)], ar_ssem.at[3 + k, 0])
        drain(gl_[k].at[pl.ds(0, NL - 1)], ar_ssem.at[3 + k, 1])
        drain(gt_[k].at[pl.ds(0, 112)], ar_ssem.at[3 + k, 2])
        with_block(k, lambda: drain(gda.at[pl.ds(0, NL - 1)], ar_ssem.at[3 + k, 3]))
    for j in range(NC):
        err_out(j).wait()
    for o in outs:
        o.wait()


def refine(ids, fill, vectors, codes, centroids, codebooks):
    anyspace = pl.BlockSpec(memory_space=pl.ANY)
    V = pltpu.VMEM
    widths = [len(g) for g in GROUPS]
    blocks = (15, 6)
    dma = pltpu.SemaphoreType.DMA
    out_shape = [
        jax.ShapeDtypeStruct((SLOTS, 768), BF),
        jax.ShapeDtypeStruct((NC, ND, 16, 256), F32),
        jax.ShapeDtypeStruct((NL, CW, CW), BF),
        jax.ShapeDtypeStruct((6, CW, CW), BF),
    ]
    scratch = (
        [
            V((NL, 1, CAP), jnp.int32), pltpu.SMEM((NL, 1, CAP), jnp.int32),
            V((4104, 8, 128), F32), V((4096, 768), BF), V((40, 8, 128), F32),
            V((NC, NL, CAP, CW), BF), V((NC, NL, CAP, CW), BF),
            V((SLOTS, 768), BF), V((NC, MC, SLOTS), jnp.int32), V((96, 8, 256), F32),
            V((NC, SLOTS, CW), BF), V((NC, CW, SLOTS), BF), V((16, SLOTS), BF), V((4, 144, 256), F32),
            V((NC, SLOTS, CW), BF),
        ]
        + [V((ND, sum_rows(g), 256), F32) for g in range(3)] * 2
        + [V((NL, 2 * w, 256), F32) for w in widths] * 2
        + [V((NL, w, 256), F32) for w in widths]
        + [V((ND, w, NL, 256), F32) for w in widths]
        + [V((ND, b, 16, CW), BF) for b in blocks] * 2
        + [V((NL, 16, CW), BF) for _ in blocks] * 2
        + [V((CW, CW), BF) for _ in blocks]
        + [V((n, CW, CW), BF) for n in (NL, 6)]
        + [dma((3,)), dma((8,)), dma((3,)), dma, dma, dma, dma, dma((NC,)), dma((5, 4)), dma((5, 4))]
    )
    return pl.pallas_call(
        refine_kernel,
        out_shape=out_shape,
        in_specs=[pl.BlockSpec(memory_space=pltpu.VMEM), pl.BlockSpec(memory_space=pltpu.SMEM)] + [anyspace] * 4,
        out_specs=[anyspace] * 4,
        scratch_shapes=scratch,
        compiler_params=pltpu.CompilerParams(
            collective_id=0, has_side_effects=True, vmem_limit_bytes=60 << 20),
    )(ids, fill, vectors, codes, centroids, codebooks)


def finish_kernel(
    err_in, books_in, ga_in, gb_in, err_out, books_out, gram_out, err, books, ga, gb, gram, in_sem, out_sem, gram_sem,
):
    parts = in_sem.shape[0] - 1
    rows = err_in.shape[0] // parts

    def pair(src, held, dst, i):
        return pltpu.make_async_copy(src, held, in_sem.at[i]), pltpu.make_async_copy(held, dst, out_sem.at[i])

    moves = []
    for i in range(parts):
        at = pl.ds(i * rows, rows)
        moves.append(pair(err_in.at[at], err.at[at], err_out.at[at], i))
    moves.append(pair(books_in, books, books_out, parts))
    loads = [pltpu.make_async_copy(ga_in, ga, gram_sem.at[0]), pltpu.make_async_copy(gb_in, gb, gram_sem.at[1])]
    for c in loads:
        c.start()
    for first, _ in moves:
        first.start()
    for c in loads:
        c.wait()
    for j in range(NC):
        for i in range(j + 1):
            block = (ga[block_of(j, i)] if j < NC - 1 else gb[i]).astype(F32)
            jr, ir = slice(j * CW, (j + 1) * CW), slice(i * CW, (i + 1) * CW)
            gram[jr, ir] = block
            if i < j:
                gram[ir, jr] = block.T
    out = pltpu.make_async_copy(gram, gram_out, gram_sem.at[0])
    out.start()
    for first, second in moves:
        first.wait()
        second.start()
    for _, second in moves:
        second.wait()
    out.wait()


def finish(err, books, ga, gb):
    anyspace = pl.BlockSpec(memory_space=pl.ANY)
    dma = pltpu.SemaphoreType.DMA
    return pl.pallas_call(
        finish_kernel,
        out_shape=[
            jax.ShapeDtypeStruct(err.shape, BF),
            jax.ShapeDtypeStruct(books.shape, F32),
            jax.ShapeDtypeStruct((768, 768), F32),
        ],
        in_specs=[anyspace] * 4,
        out_specs=[anyspace] * 3,
        scratch_shapes=[
            pltpu.VMEM(err.shape, BF), pltpu.VMEM(books.shape, F32),
            pltpu.VMEM(ga.shape, BF), pltpu.VMEM(gb.shape, BF), pltpu.VMEM((768, 768), F32),
            dma((9,)), dma((9,)), dma((2,)),
        ],
        compiler_params=pltpu.CompilerParams(vmem_limit_bytes=60 << 20),
    )(err, books, ga, gb)


def local(vectors, list_ids, codes, fill_counts, centroids, codebooks):
    codes_t = codes.T.reshape(NC, MC, SLOTS)
    err, books, ga, gb = refine(
        list_ids.reshape(NL, 1, CAP), fill_counts, vectors, codes_t, centroids, codebooks)
    err, books, gram = finish(err, books, ga, gb)
    return err, books.reshape(96, 8, 256), gram


def solution(mesh):
    in_specs = (
        P(("dp", "list"), None),
        P(("dp", "list")),
        P(("dp", "list"), None),
        P(("dp", "list"), None),
        P("list", None),
        P(),
    )
    out_specs = (P(("dp", "list"), None), P(), P())
    return jax.shard_map(local, mesh=mesh, in_specs=in_specs, out_specs=out_specs, check_vma=False)
```
